512 devices in a mesh: expert: 128 (over x, z, core), dp: 4 (over y).
Axes of the slice: x: 4, y: 4, z: 16, core: 2. Of those that a mesh axis runs over, the one named last changes fastest.
Arguments:
- tokens_in: bfloat16 [16384, 3584], P('expert', 'dp'), may hold values from -6 to 6
- out_grad: bfloat16 [16384, 3584], P('expert', 'dp'), may hold values from -0.31 to 0.31
- expert_ids: int32 [16384, 8], P('expert'), may hold values from 0 to 383, all different within a row; in each aligned block of 128 rows (0 to 127, 128 to 255, ...) at most 6 rows name the same one
- combine: bfloat16 [16384, 8], P('expert'), may hold values from 0.049804688 to 0.5
- down_weight: bfloat16 [128, 1024, 3584], P('expert', 'dp'), may hold values from -2 to 2
- gate_saved: bfloat16 [128, 768, 1024], P('expert', None, 'dp'), may hold values from -6 to 6
- up_saved: bfloat16 [128, 768, 1024], P('expert', None, 'dp'), may hold values from -6 to 6
Outputs:
- update: bfloat16 [128, 3584, 1024], P('expert', 'dp')
- dcombine: float32 [16384, 8], P('expert')
The draws below stay inside these ranges and needn't reach their ends.
Inputs may be any that keep to these rules, and one draw needn't show every extreme that they name: `expert_ids`: each row names 8 different experts. In each aligned block of 128 rows no expert is named by more than 6 rows, a bound that some block reaches.
All inputs are finite; a program needn't handle non-finite values.
Results may differ from the reference program's by a relative error of at most 0.018.
Values may be sent and summed in bfloat16 or wider, within the bound.
No kernel may reach another device: no remote copies, remote signals or barrier semaphores. Data moves between devices by JAX's collectives and lax.ppermute only.
A program may use at most 64 MiB of HBM per device.

```python
import math
import jax
import jax.numpy as jnp
import numpy as np
from jax import lax

D = 3584
F = 1024
TOP = 8
TOK_DEV = 128
EXPERTS = 384
TOKENS = 16384
CAP = 6
SLOTS = 768
N_EXPERT = 128
N_DP = 4


def column_rise(count, base_scale, growth):
    column = jnp.arange(count, dtype=jnp.float32) / count
    return base_scale * jnp.exp(math.log(growth) * column)


def draw_tokens_in(key, part):
    key = jax.random.fold_in(key, 2)
    noise = jax.random.normal(key, (TOKENS, D), jnp.float32)
    field = noise * column_rise(D, 0.6, 3.0)[None, :]
    return jnp.clip(field, -6.0, 6.0).astype(jnp.bfloat16)


def draw_out_grad(key, part):
    key = jax.random.fold_in(key, 3)
    noise = jnp.clip(jax.random.normal(key, (TOKENS, D), jnp.float32), -6.0, 6.0)
    return (0.05 * noise).astype(jnp.bfloat16)


def draw_down_weight(key, part):
    key = jax.random.fold_in(key, 5)
    value_key = jax.random.fold_in(key, 1)
    factor_key = jax.random.fold_in(key, 2)
    half_range = 0.5 * math.log(3.0)
    factor = jnp.exp(jax.random.uniform(factor_key, (N_EXPERT, F, 1), jnp.float32, -half_range, half_range))
    values = jnp.clip(jax.random.normal(value_key, (N_EXPERT, F, D), jnp.float32), -3.0, 3.0)
    rise = column_rise(F, 1.0 / math.sqrt(2.5), 2.5)
    scale = rise[None, :, None] * factor / math.sqrt(F)
    return (values * scale).astype(jnp.bfloat16)


def levels(own_key, extent, split, low, top_value):
    loudness, own = 1.0, jax.random.fold_in(own_key, 6)
    for dim, blocks in split:
        draws = jnp.exp(jax.random.uniform(jax.random.fold_in(own, dim), (blocks,), jnp.float32, low / len(split), top_value / len(split)))
        loudness = loudness * jnp.repeat(draws, extent[dim] // blocks).reshape([-1 if axis == dim else 1 for axis in range(len(extent))])
    return loudness


def assign_block(rng, own, number, rows, count, top, most, skew):
    sequence = jax.random.permutation(rng, count)
    crowded, common = shares(count, rows * top, most, skew, True), shares(count, rows * top, most, skew, False)
    places = jnp.arange(count)

    def named(sizes, turn):
        used = int((sizes > 0).sum())
        fixed = max(1, used // 4)
        moved = fixed + (places - fixed + turn * (used - fixed)) % max(1, count - fixed)
        return jnp.zeros((count,), jnp.int32).at[sequence[jnp.where(places < fixed, places, moved)]].set(jnp.asarray(sizes, jnp.int32))

    sizes = jnp.where(number % 4 == 0, named(crowded, number // 4), named(common, number - number // 4 - 1))
    mixed = jax.random.permutation(jax.random.fold_in(own, 3), count)
    giver, sink = mixed[0:count // 2 * 2:2], mixed[1:count // 2 * 2:2]
    room = jnp.minimum(sizes[giver] - 1, most - sizes[sink]) // 2
    room = jnp.where((giver == sequence[0]) | (sink == sequence[0]) | (sizes[sink] == 0), 0, jnp.maximum(room, 0))
    moved = jax.random.randint(jax.random.fold_in(own, 4), (count // 2,), 0, 1 << 20) % (room + 1)
    sizes = sizes.at[giver].add(-moved).at[sink].add(moved)
    labels = jnp.searchsorted(jnp.cumsum(sizes), jnp.arange(rows * top), side="right").astype(jnp.int32)
    listing = labels.reshape(top, rows).T
    listing = listing[jax.random.permutation(jax.random.fold_in(own, 1), rows)]
    turn = jax.random.randint(jax.random.fold_in(own, 2), (rows, 1), 0, top)
    return jnp.take_along_axis(listing, (jnp.arange(top)[None, :] + turn) % top, axis=1)


def shares(number_of, total, most, slope, full):
    loads = [(1 << 20) // math.isqrt(standing ** slope) + 1 for standing in range(1, number_of + 1)]
    largest = most if full else min(most, max(-(-total // number_of), total * loads[0] // sum(loads)))
    least = 1 if total - largest >= number_of - 1 else 0
    holding, spare = [largest] + [least] * (number_of - 1), total - largest - least * (number_of - 1)
    while spare > 0:
        candidates = [i for i in range(1, number_of) if holding[i] < largest] or [i for i in range(1, number_of) if holding[i] < most]
        pool, left = sum([loads[i] for i in candidates]), spare
        for i in candidates:
            addition = min(most - holding[i], max(1, left * loads[i] // pool), spare)
            holding[i] = holding[i] + addition
            spare = spare - addition
    return np.array(holding)


def bell_draw(own_key, shape, deviation, limit, cuts=(), kind=jnp.bfloat16):
    gain = levels(own_key, shape, cuts, -0.22, 0.18) if cuts else 1.0
    values = jax.random.normal(own_key, shape, jnp.float32) * deviation * gain
    return jnp.minimum(jnp.maximum(values, -limit), limit).astype(kind)


def setup_inputs(seed: int = 0) -> dict:
    seeds = jax.random.split(jax.random.key(seed), 8)
    tokens_in = draw_tokens_in(jax.random.fold_in(seeds[7], 71), 0)
    out_grad = draw_out_grad(jax.random.fold_in(seeds[7], 71), 0)
    expert_ids_keys = jax.random.split(jax.random.fold_in(seeds[2], 1), TOKENS // TOK_DEV)
    expert_ids_turns = jax.random.permutation(jax.random.fold_in(seeds[2], 3), TOKENS // TOK_DEV)
    expert_ids = jax.vmap(lambda own, number: assign_block(jax.random.fold_in(seeds[2], 2), own, number, TOK_DEV, EXPERTS, TOP, CAP, 2))(expert_ids_keys, expert_ids_turns).reshape((TOKENS, TOP))
    combine = jnp.clip(0.049804688 + 0.4501953 * jax.random.uniform(seeds[3], (TOKENS, TOP), jnp.float32) ** levels(seeds[3], (TOKENS, TOP), ((0, 128),), -0.2, 0.2), 0.049804688, 0.5).astype(jnp.bfloat16)
    down_weight = draw_down_weight(jax.random.fold_in(seeds[7], 71), 0)
    gate_saved = bell_draw(seeds[5], (N_EXPERT, SLOTS, F), 1.0, 6.0, ((0, 128), (2, 4)))
    up_saved = bell_draw(seeds[6], (N_EXPERT, SLOTS, F), 1.0, 6.0, ((0, 128), (2, 4)))
    return dict(tokens_in=tokens_in, out_grad=out_grad, expert_ids=expert_ids, combine=combine, down_weight=down_weight, gate_saved=gate_saved, up_saved=up_saved)


poly_first = 8.28721201814563
poly_third = -23.595886519098837
poly_fifth = 17.300387312530933

def block_positions(block_routes):
    flat_ids = block_routes.reshape(-1)
    pair_count = flat_ids.shape[0]
    same_id = flat_ids[:, None] == flat_ids[None, :]
    earlier = jnp.arange(pair_count)[None, :] < jnp.arange(pair_count)[:, None]
    return lax.optimization_barrier(jnp.sum(jnp.logical_and(same_id, earlier), axis=1)).astype(jnp.int32)

def reference(tokens_in, out_grad, expert_ids, combine, down_weight, gate_saved, up_saved):
    blocks = expert_ids.reshape(N_EXPERT, TOK_DEV * TOP)
    positions = lax.map(block_positions, blocks).reshape(TOKENS, TOP)
    source = (jnp.arange(TOKENS, dtype=jnp.int32) // TOK_DEV)[:, None]
    slot_of = source * CAP + positions
    is_live = expert_ids < N_EXPERT
    flat_index = jnp.where(is_live, expert_ids * SLOTS + slot_of, N_EXPERT * SLOTS).astype(jnp.int32)
    token_index = jnp.broadcast_to(jnp.arange(TOKENS, dtype=jnp.int32)[:, None], (TOKENS, TOP))
    inverse = jnp.full((N_EXPERT * SLOTS,), TOKENS, jnp.int32).at[flat_index.reshape(-1)].set(token_index.reshape(-1), mode='drop')
    slot_weight = jnp.zeros((N_EXPERT * SLOTS,), jnp.float32).at[flat_index.reshape(-1)].set(combine.reshape(-1).astype(jnp.float32), mode='drop')
    padded_grad = jnp.concatenate([out_grad, jnp.zeros((1, D), out_grad.dtype)], 0)
    padded_tokens = jnp.concatenate([tokens_in, jnp.zeros((1, D), tokens_in.dtype)], 0)

    def one_expert(operands):
        rows, weights, matrix, gate_pre, up_pre = operands
        grad_rows = padded_grad[rows]
        token_rows = padded_tokens[rows]
        hidden_grad = jnp.dot(grad_rows, matrix.T, preferred_element_type=jnp.float32)
        gate_act = jax.nn.silu(gate_pre.astype(jnp.float32))
        hidden_act = gate_act * up_pre.astype(jnp.float32)
        weight_grad = lax.optimization_barrier(jnp.sum(hidden_grad * hidden_act, axis=1))
        up_grad = (weights[:, None] * hidden_grad * gate_act).astype(jnp.bfloat16)
        gradient = jnp.dot(token_rows.T, up_grad, preferred_element_type=jnp.float32)
        frobenius = jnp.sqrt(jnp.sum(gradient * gradient))
        start_iter = (gradient / (1.01 * frobenius + 1e-07)).astype(jnp.bfloat16)
        shards = start_iter.astype(jnp.float32).reshape(N_DP, D // N_DP, F)
        partial_grams = jnp.einsum('qdf,qdg->qfg', shards, shards, precision=lax.Precision.HIGHEST)
        gram = lax.optimization_barrier(jnp.sum(partial_grams.astype(jnp.bfloat16).astype(jnp.float32), axis=0))
        gram_low = gram.astype(jnp.bfloat16)
        square = jnp.dot(gram_low, gram_low, preferred_element_type=jnp.float32)
        quartic = jnp.sum(square * square)
        bound = jnp.sqrt(jnp.sqrt(quartic)) + 1e-06
        first_scale = poly_third / bound
        second_scale = poly_fifth / (bound * bound)
        poly = (first_scale * gram_low.astype(jnp.float32) + second_scale * square).astype(jnp.bfloat16)
        mixed = jnp.dot(start_iter, poly, preferred_element_type=jnp.float32)
        update = (math.sqrt(D) * (poly_first * start_iter.astype(jnp.float32) + mixed)).astype(jnp.bfloat16)
        return (update, weight_grad)
    updates, weight_grads = lax.map(one_expert, (inverse.reshape(N_EXPERT, SLOTS), slot_weight.reshape(N_EXPERT, SLOTS), down_weight, gate_saved, up_saved))
    values = weight_grads.reshape(-1)
    picked = values[jnp.minimum(flat_index, N_EXPERT * SLOTS - 1)]
    dcombine = jnp.where(is_live, picked, jnp.float32(0.0))
    return (updates, dcombine)
```

```python
import math

import jax
import jax.numpy as jnp
from jax import lax
from jax.sharding import Mesh
from jax.sharding import PartitionSpec as P

D = 3584
CAP = 6
PLANE = (4, 16, 2)

poly_first = 8.28721201814563
poly_third = -23.595886519098837
poly_fifth = 17.300387312530933

f32, bf16 = jnp.float32, jnp.bfloat16


def dot(a, b, contract):
    return lax.dot_general(a, b, (contract, ((), ())), preferred_element_type=f32)


def block_positions(flat_ids):
    pair_count = flat_ids.shape[0]
    same_id = flat_ids[:, None] == flat_ids[None, :]
    earlier = jnp.arange(pair_count)[None, :] < jnp.arange(pair_count)[:, None]
    return jnp.sum(jnp.logical_and(same_id, earlier), axis=1)


def shift(values, step):
    size = lax.axis_size("y")
    return lax.ppermute(values, "y", [(i, (i + step) % size) for i in range(size)])


def gather_weights(own):
    size, rank = lax.axis_size("y"), lax.axis_index("y")
    half = own.shape[0] // 2
    before = shift(own, 1)
    after = shift(own, -1)
    far_low = shift(before[:half], 1)
    far_high = shift(after[half:], -1)
    whole = jnp.zeros((size,) + own.shape, own.dtype)
    parts = ((own, 0, 0), (before, -1, 0), (after, 1, 0), (far_low, 2, 0), (far_high, 2, half))
    for part, step, row in parts:
        place = lax.rem(rank + size + step, size)
        whole = lax.dynamic_update_slice(whole, part[None], (place, row, 0))
    return whole.reshape(size * own.shape[0], own.shape[1])


def on_device(tokens_in, out_grad, expert_ids, combine, down_weight, gate_saved, up_saved):
    nx, nz, nc = (lax.axis_size(name) for name in ("x", "z", "c"))
    ny = lax.axis_size("y")
    experts = nx * nz * nc
    near = nx * nc
    zl = nz // ny
    slots = experts * CAP
    own_slots = slots // ny
    tok_rows, top_count = expert_ids.shape
    feats = tokens_in.shape[1]
    hidden_part = gate_saved.shape[2]
    hidden_all = hidden_part * ny

    column = lax.all_gather(
        jnp.concatenate([tokens_in, out_grad], axis=1), "z", axis=0, tiled=True
    )
    matrix = gather_weights(down_weight[0])

    flat_ids = expert_ids.reshape(-1)
    position = block_positions(flat_ids)
    is_live = flat_ids < experts
    ez = (flat_ids // nc) % nz
    exc = (flat_ids // (nc * nz)) * nc + flat_ids % nc
    target = jnp.where(is_live, (ez * near + exc) * CAP + position, -1)
    matches = target[None, :] == jnp.arange(slots, dtype=jnp.int32)[:, None]
    token_of = (jnp.arange(tok_rows * top_count, dtype=jnp.int32) // top_count).astype(f32) + 1.0
    index_send = jnp.sum(jnp.where(matches, token_of[None, :], 0.0), axis=1)
    weight_send = jnp.sum(
        jnp.where(matches, combine.astype(f32).reshape(1, -1), 0.0), axis=1
    )
    routes = lax.all_to_all(
        jnp.stack([index_send.reshape(nz, near * CAP), weight_send.reshape(nz, near * CAP)], 1),
        "z", 0, 0, tiled=True,
    )
    routes = routes.reshape(nz, 2, near, CAP)
    start = (jnp.arange(nz, dtype=jnp.int32) * tok_rows).astype(f32)[:, None, None]
    index = jnp.where(routes[:, 0] > 0.0, routes[:, 0] + start, 0.0)
    split = index.reshape(ny, zl, near, CAP)
    index_tok = index.transpose(1, 0, 2).reshape(-1)
    index_grad = split.transpose(0, 2, 1, 3).reshape(-1)
    columns = (jnp.arange(nz * tok_rows, dtype=jnp.int32) + 1).astype(f32)
    select_tok = (index_tok[:, None] == columns[None, :]).astype(bf16)
    select_grad = (index_grad[:, None] == columns[None, :]).astype(bf16)
    weight_order = routes[:, 1].reshape(ny, zl, near, CAP).transpose(0, 2, 1, 3)
    weight = lax.all_to_all(
        weight_order.reshape(ny * near, zl * CAP), ("y", "x", "c"), 0, 0, tiled=True
    )
    weight = weight.reshape(ny, own_slots)[0]

    row = jnp.arange(slots, dtype=jnp.int32)
    rest = row // CAP
    block = rest % zl
    rest = rest // zl
    row_c = rest % nc
    rest = rest // nc
    row_x = rest % nx
    row_q = rest // nx
    source = ((row_x * nz + row_q * zl + block) * nc + row_c) * CAP + row % CAP
    order = (source[:, None] == row[None, :]).astype(bf16)
    saved = jnp.concatenate([gate_saved[0], up_saved[0]], axis=1)
    saved = dot(order, saved, ((1,), (0,))).astype(bf16)
    saved = lax.all_to_all(
        saved.reshape(ny, own_slots, 2 * hidden_part), "y", 0, 0, tiled=True
    )
    gate = saved[:, :, :hidden_part].transpose(1, 0, 2).reshape(own_slots, hidden_all)
    up = saved[:, :, hidden_part:].transpose(1, 0, 2).reshape(own_slots, hidden_all)
    gate_act = jax.nn.silu(gate.astype(f32))
    hidden_act = gate_act * up.astype(f32)

    rows = dot(select_tok, column[:, :feats], ((1,), (0,))).astype(bf16)
    rows = lax.all_to_all(
        rows.reshape(near, nz * CAP, feats), ("x", "c"), 0, 0, tiled=True
    )
    rows = rows.reshape(near, ny, zl * CAP, feats).transpose(1, 0, 2, 3).reshape(slots, feats)
    inner = lax.psum(dot(rows, rows, ((1,), (1,))).astype(bf16), "y")

    grads = dot(select_grad, column[:, feats:], ((1,), (0,))).astype(bf16)
    grads = lax.all_to_all(
        grads.reshape(ny * near, zl * CAP, feats), ("y", "x", "c"), 0, 0, tiled=True
    )
    grads = grads.reshape(ny, own_slots, feats).transpose(1, 0, 2).reshape(own_slots, ny * feats)
    hidden_grad = dot(grads, matrix, ((1,), (1,)))
    slot_dw = jnp.sum(hidden_grad * hidden_act, axis=1)
    up_own = (weight[:, None] * hidden_grad * gate_act).astype(bf16)
    up_grad = lax.all_to_all(
        jnp.broadcast_to(up_own[None], (ny, own_slots, hidden_all)), "y", 0, 0, tiled=True
    ).reshape(slots, hidden_all)

    back = jnp.broadcast_to(slot_dw.reshape(1, near, zl * CAP), (ny, near, zl * CAP))
    back = lax.all_to_all(
        back.reshape(ny * near, zl * CAP), ("y", "x", "c"), 0, 0, tiled=True
    )
    back = back.reshape(ny, near, zl, CAP).transpose(0, 2, 1, 3).reshape(nz, near * CAP)
    back = lax.all_to_all(back, "z", 0, 0, tiled=True).reshape(-1)
    dcombine = jnp.sum(jnp.where(matches, back[:, None], 0.0), axis=0)
    dcombine = dcombine.reshape(tok_rows, top_count)

    gradient = dot(rows, up_grad, ((0,), (0,)))
    carried = dot(inner, up_grad, ((1,), (0,)))
    norm_total = jnp.sum(carried * up_grad.astype(f32))
    scale = 1.0 / (1.01 * jnp.sqrt(jnp.maximum(norm_total, 0.0)) + 1e-07)
    gram = dot(up_grad, carried.astype(bf16), ((0,), (0,)))
    gram_low = (gram * scale * scale).astype(bf16)
    start_iter = (gradient * scale).astype(bf16)
    square = dot(gram_low, gram_low, ((1,), (0,)))
    quartic = jnp.sum(square * square)
    bound = jnp.sqrt(jnp.sqrt(quartic)) + 1e-06
    first_scale = poly_third / bound
    second_scale = poly_fifth / (bound * bound)
    poly = (first_scale * gram_low.astype(f32) + second_scale * square).astype(bf16)
    mixed = dot(start_iter, poly, ((1,), (0,)))
    update = (math.sqrt(D) * (poly_first * start_iter.astype(f32) + mixed)).astype(bf16)
    return (update[None], dcombine)


def build(mesh, plane):
    split_mesh = Mesh(
        mesh.devices.reshape(plane + (mesh.devices.shape[1],)), ("x", "z", "c", "y")
    )
    expert = ("x", "z", "c")
    in_specs = (
        P(expert, "y"),
        P(expert, "y"),
        P(expert, None),
        P(expert, None),
        P(expert, "y", None),
        P(expert, None, "y"),
        P(expert, None, "y"),
    )
    out_specs = (P(expert, "y", None), P(expert, None))
    return jax.shard_map(
        on_device, mesh=split_mesh, in_specs=in_specs, out_specs=out_specs, check_vma=False
    )


def solution(mesh):
    return build(mesh, PLANE)
```

```python
import math

import jax
import jax.numpy as jnp
from jax import lax
from jax.experimental import pallas as pl
from jax.experimental.pallas import tpu as pltpu
from jax.sharding import Mesh
from jax.sharding import PartitionSpec as P

D = 3584
CAP = 6
PLANE = (4, 16, 2)

poly_first = 8.28721201814563
poly_third = -23.595886519098837
poly_fifth = 17.300387312530933

f32, bf16 = jnp.float32, jnp.bfloat16
VMEM = 48 * 1024 * 1024


def dot(a, b, contract):
    return lax.dot_general(a, b, (contract, ((), ())), preferred_element_type=f32)


def block_positions(flat_ids):
    pair_count = flat_ids.shape[0]
    same_id = flat_ids[:, None] == flat_ids[None, :]
    earlier = jnp.arange(pair_count)[None, :] < jnp.arange(pair_count)[:, None]
    return jnp.sum(jnp.logical_and(same_id, earlier), axis=1)


def shift(values, step):
    size = lax.axis_size("y")
    return lax.ppermute(values, "y", [(i, (i + step) % size) for i in range(size)])


def gather_weights(own):
    size, rank = lax.axis_size("y"), lax.axis_index("y")
    half = own.shape[0] // 2
    before = shift(own, 1)
    after = shift(own, -1)
    far_low = shift(before[:half], 1)
    far_high = shift(after[half:], -1)
    whole = jnp.zeros((size,) + own.shape, own.dtype)
    parts = ((own, 0, 0), (before, -1, 0), (after, 1, 0), (far_low, 2, 0), (far_high, 2, half))
    for part, step, row in parts:
        place = lax.rem(rank + size + step, size)
        whole = lax.dynamic_update_slice(whole, part[None], (place, row, 0))
    return whole


def total(values):
    return jnp.sum(jnp.sum(values, axis=0, keepdims=True), axis=1, keepdims=True)


def swap(values, partner):
    size = lax.axis_size("y")
    return lax.ppermute(values, "y", [(i, partner(i)) for i in range(size)])


def pick_kernel(index_ref, column_ref, tok_ref, grad_ref):
    near, _, rows, feats = tok_ref.shape
    count = column_ref.shape[1]
    columns = lax.broadcasted_iota(jnp.int32, (near * rows, count), 1).astype(f32) + 1.0
    chosen = jnp.where(index_ref[0] == columns, 1.0, 0.0).astype(bf16)
    for part, out in ((0, tok_ref), (1, grad_ref)):
        values = column_ref[0, :, part * feats : (part + 1) * feats]
        picked = dot(chosen, values, ((1,), (0,))).reshape(near, rows, feats).astype(bf16)
        if part:
            out[0] = picked
        else:
            out[:, 0] = picked


def pick_rows(index, column, near):
    quarters, rows, _ = index.shape
    feats = column.shape[2] // 2
    piece = rows // near
    return pl.pallas_call(
        pick_kernel,
        grid=(quarters,),
        in_specs=[
            pl.BlockSpec((1, rows, 1), lambda q: (q, 0, 0)),
            pl.BlockSpec((1,) + column.shape[1:], lambda q: (q, 0, 0)),
        ],
        out_specs=[
            pl.BlockSpec((near, 1, piece, feats), lambda q: (0, q, 0, 0)),
            pl.BlockSpec((1, near, piece, feats), lambda q: (q, 0, 0, 0)),
        ],
        out_shape=[
            jax.ShapeDtypeStruct((near, quarters, piece, feats), bf16),
            jax.ShapeDtypeStruct((quarters, near, piece, feats), bf16),
        ],
        compiler_params=pltpu.CompilerParams(vmem_limit_bytes=VMEM),
        name="pick_rows",
    )(index, column)


def inner_kernel(recv_ref, rows_t_ref, low_ref, high_ref, rows_ref):
    near, quarters, piece, feats = recv_ref.shape
    own = near * piece
    for q in range(quarters):
        rows_ref[q * own : (q + 1) * own] = (
            recv_ref[:, q].astype(f32).reshape(own, feats).astype(bf16)
        )
    half = quarters * own // 2
    top, end = rows_ref[:half], rows_ref[half:]
    low_ref[:half] = dot(top, top, ((1,), (1,))).astype(bf16)
    cross = dot(top, end, ((1,), (1,))).astype(bf16)
    low_ref[half:] = cross[: half // 2]
    high_ref[: half // 2] = cross[half // 2 :]
    high_ref[half // 2 :] = dot(end, end, ((1,), (1,))).astype(bf16)
    rows_t_ref[...] = rows_ref[...].T


def inner_products(recv):
    near, quarters, piece, feats = recv.shape
    slots = near * quarters * piece
    half = slots // 2
    pack = jax.ShapeDtypeStruct((half + half // 2, half), bf16)
    return pl.pallas_call(
        inner_kernel,
        out_shape=[jax.ShapeDtypeStruct((feats, slots), bf16), pack, pack],
        scratch_shapes=[pltpu.VMEM((slots, feats), bf16)],
        compiler_params=pltpu.CompilerParams(vmem_limit_bytes=VMEM),
        name="inner_products",
    )(recv)


def hidden_kernel(grads_ref, matrix_ref, saved_ref, weight_ref, up_ref, dw_ref):
    parts, rows, feats = grads_ref.shape
    width = matrix_ref.shape[1]
    hidden = jnp.zeros((rows, width), f32)
    for part in range(parts):
        block = matrix_ref[0, :, part * feats : (part + 1) * feats]
        hidden = hidden + dot(grads_ref[part], block, ((1,), (1,)))
    gate = saved_ref[0, :, :width].astype(f32)
    up = saved_ref[0, :, width:].astype(f32)
    act = gate / (1.0 + jnp.exp(-gate))
    scaled = hidden * act
    up_ref[...] = (weight_ref[...] * scaled).astype(bf16)
    share = jnp.sum(scaled * up, axis=1, keepdims=True)

    @pl.when(pl.program_id(0) == 0)
    def _():
        dw_ref[...] = share

    @pl.when(pl.program_id(0) != 0)
    def _():
        dw_ref[...] += share


def hidden_step(grads, matrix, saved, weight):
    parts, rows, feats = grads.shape
    blocks, width, depth = matrix.shape
    return pl.pallas_call(
        hidden_kernel,
        grid=(blocks,),
        in_specs=[
            pl.BlockSpec((parts, rows, feats), lambda j: (0, 0, 0)),
            pl.BlockSpec((1, width, depth), lambda j: (j, 0, 0)),
            pl.BlockSpec((1, rows, 2 * width), lambda j: (j, 0, 0)),
            pl.BlockSpec((rows, 1), lambda j: (0, 0)),
        ],
        out_specs=[
            pl.BlockSpec((rows, width), lambda j: (0, j)),
            pl.BlockSpec((rows, 1), lambda j: (0, 0)),
        ],
        out_shape=[
            jax.ShapeDtypeStruct((rows, blocks * width), bf16),
            jax.ShapeDtypeStruct((rows, 1), f32),
        ],
        compiler_params=pltpu.CompilerParams(vmem_limit_bytes=VMEM),
        name="hidden_step",
    )(grads, matrix, saved, weight)


def last_kernel(
    rank_ref, rows_t_ref, low_a, low_b, high_a, high_b, up_0, up_1, up_2, up_3, out_ref,
    up_ref, inner_ref, carried_ref, gram_ref, square_ref, poly_ref, start_ref,
):
    rank = rank_ref[0]
    own = up_0.shape[0]
    slots, hidden = up_ref.shape
    feats = rows_t_ref.shape[0]
    half = slots // 2
    for step, part in ((0, up_0), (3, up_1), (1, up_2), (2, up_3)):
        place = pl.multiple_of(lax.rem(rank + step, 4) * own, own)
        up_ref[pl.ds(place, own)] = part[...]
    low = low_a[...].astype(f32) + low_b[...].astype(f32)
    high = high_a[...].astype(f32) + high_b[...].astype(f32)
    inner_ref[:half, :half] = low[:half].astype(bf16)
    inner_ref[half:, half:] = high[half // 2 :].astype(bf16)
    cross = jnp.concatenate([low[half:], high[: half // 2]], axis=0)
    inner_ref[:half, half:] = cross.astype(bf16)
    inner_ref[half:, :half] = cross.T.astype(bf16)
    norm = jnp.zeros((1, 1), f32)
    step = slots // 3
    for i in range(0, slots, step):
        carried = dot(inner_ref[i : i + step], up_ref[...], ((1,), (0,)))
        norm = norm + total(carried * up_ref[i : i + step].astype(f32))
        carried_ref[i : i + step] = carried.astype(bf16)
    scale = 1.0 / (1.01 * jnp.sqrt(jnp.maximum(norm, 0.0)) + 1e-07)
    step = hidden // 4
    for i in range(0, hidden, step):
        gram = dot(up_ref[:, i : i + step], carried_ref[...], ((0,), (0,)))
        gram_ref[i : i + step] = (gram * scale * scale).astype(bf16)
    quartic = jnp.zeros((1, 1), f32)
    for i in range(0, hidden, step):
        square = dot(gram_ref[i : i + step], gram_ref[...], ((1,), (0,)))
        quartic = quartic + total(square * square)
        square_ref[i : i + step] = square
    rows = feats // 4
    for i in range(0, feats, rows):
        gradient = dot(rows_t_ref[i : i + rows], up_ref[...], ((1,), (0,)))
        start_ref[i : i + rows] = (gradient * scale).astype(bf16)
    bound = jnp.sqrt(jnp.sqrt(quartic)) + 1e-06
    first_scale = poly_third / bound
    second_scale = poly_fifth / (bound * bound)
    for i in range(0, hidden, step):
        poly_ref[i : i + step] = (
            first_scale * gram_ref[i : i + step].astype(f32)
            + second_scale * square_ref[i : i + step]
        ).astype(bf16)
    for i in range(0, feats, rows):
        start = start_ref[i : i + rows]
        mixed = dot(start, poly_ref[...], ((1,), (0,)))
        out_ref[0, i : i + rows] = (
            math.sqrt(D) * (poly_first * start.astype(f32) + mixed)
        ).astype(bf16)


def last_step(rank, rows_t, packs, ups):
    feats, slots = rows_t.shape
    hidden = ups[0].shape[1]
    vmem = pl.BlockSpec(memory_space=pltpu.VMEM)
    return pl.pallas_call(
        last_kernel,
        in_specs=[pl.BlockSpec(memory_space=pltpu.SMEM)] + [vmem] * 9,
        out_specs=vmem,
        out_shape=jax.ShapeDtypeStruct((1, feats, hidden), bf16),
        scratch_shapes=[
            pltpu.VMEM((slots, hidden), bf16),
            pltpu.VMEM((slots, slots), bf16),
            pltpu.VMEM((slots, hidden), bf16),
            pltpu.VMEM((hidden, hidden), bf16),
            pltpu.VMEM((hidden, hidden), f32),
            pltpu.VMEM((hidden, hidden), bf16),
            pltpu.VMEM((feats, hidden), bf16),
        ],
        compiler_params=pltpu.CompilerParams(vmem_limit_bytes=VMEM),
        name="last_step",
    )(rank, rows_t, *packs, *ups)


def on_device(tokens_in, out_grad, expert_ids, combine, down_weight, gate_saved, up_saved):
    nx, nz, nc = (lax.axis_size(name) for name in ("x", "z", "c"))
    ny = lax.axis_size("y")
    experts = nx * nz * nc
    near = nx * nc
    zl = nz // ny
    slots = experts * CAP
    own_slots = slots // ny
    tok_rows, top_count = expert_ids.shape
    feats = tokens_in.shape[1]
    hidden_part = gate_saved.shape[2]

    column = lax.all_gather(
        jnp.concatenate([tokens_in, out_grad], axis=1), "z", axis=0, tiled=True
    )
    matrix = gather_weights(down_weight[0])

    flat_ids = expert_ids.reshape(-1)
    position = block_positions(flat_ids)
    is_live = flat_ids < experts
    ez = (flat_ids // nc) % nz
    exc = (flat_ids // (nc * nz)) * nc + flat_ids % nc
    target = jnp.where(is_live, (ez * near + exc) * CAP + position, -1)
    matches = target[None, :] == jnp.arange(slots, dtype=jnp.int32)[:, None]
    token_of = (jnp.arange(tok_rows * top_count, dtype=jnp.int32) // top_count).astype(f32) + 1.0
    index_send = jnp.sum(jnp.where(matches, token_of[None, :], 0.0), axis=1)
    weight_send = jnp.sum(
        jnp.where(matches, combine.astype(f32).reshape(1, -1), 0.0), axis=1
    )
    routes = lax.all_to_all(
        jnp.stack([index_send.reshape(nz, near * CAP), weight_send.reshape(nz, near * CAP)], 1),
        "z", 0, 0, tiled=True,
    )
    routes = routes.reshape(nz, 2, near, CAP)
    start = (jnp.arange(nz, dtype=jnp.int32) % zl * tok_rows).astype(f32)[:, None, None]
    index = jnp.where(routes[:, 0] > 0.0, routes[:, 0] + start, 0.0)
    index = index.reshape(ny, zl, near, CAP).transpose(0, 2, 1, 3).reshape(ny, own_slots, 1)
    weight_order = routes[:, 1].reshape(ny, zl, near, CAP).transpose(0, 2, 1, 3)
    weight = lax.all_to_all(
        weight_order.reshape(ny * near, zl * CAP), ("y", "x", "c"), 0, 0, tiled=True
    )
    weight = weight.reshape(ny, own_slots)[0][:, None]

    row = jnp.arange(slots, dtype=jnp.int32)
    rest = row // CAP
    block = rest % zl
    rest = rest // zl
    row_c = rest % nc
    rest = rest // nc
    row_x = rest % nx
    row_q = rest // nx
    source = ((row_x * nz + row_q * zl + block) * nc + row_c) * CAP + row % CAP
    order = (source[:, None] == row[None, :]).astype(bf16)
    saved = jnp.concatenate([gate_saved[0], up_saved[0]], axis=1)
    saved = dot(order, saved, ((1,), (0,))).astype(bf16)
    saved = lax.all_to_all(
        saved.reshape(ny, own_slots, 2 * hidden_part), "y", 0, 0, tiled=True
    )

    column, matrix, saved = lax.optimization_barrier((column, matrix, saved))
    token_send, grad_send = pick_rows(
        index, column.reshape(ny, zl * tok_rows, 2 * feats), near
    )
    rows = lax.all_to_all(
        token_send.reshape(near, nz * CAP, feats), ("x", "c"), 0, 0, tiled=True
    ).reshape(near, ny, zl * CAP, feats)
    rows_t, low, high = inner_products(rows)
    beside, across = (lambda i: i ^ 1), (lambda i: ny - 1 - i)
    low_near, high_near = swap(low, beside), swap(high, across)

    grad_send, _ = lax.optimization_barrier((grad_send, rows))
    grads = lax.all_to_all(
        grad_send.reshape(ny * near, zl * CAP, feats), ("y", "x", "c"), 0, 0, tiled=True
    ).reshape(ny, own_slots, feats)
    low_near, high_near, grads = lax.optimization_barrier((low_near, high_near, grads))
    low, high = low + low_near, high + high_near
    packs = (low, swap(low, across), high, swap(high, beside))
    up_own, slot_dw = hidden_step(grads, matrix, saved, weight)
    ups = (up_own, shift(up_own, 1), shift(up_own, -1), shift(up_own, 2))

    back = jnp.broadcast_to(slot_dw.reshape(1, near, zl * CAP), (ny, near, zl * CAP))
    back = lax.all_to_all(
        back.reshape(ny * near, zl * CAP), ("y", "x", "c"), 0, 0, tiled=True
    )
    back = back.reshape(ny, near, zl, CAP).transpose(0, 2, 1, 3).reshape(nz, near * CAP)
    back = lax.all_to_all(back, "z", 0, 0, tiled=True).reshape(-1)
    dcombine = jnp.sum(jnp.where(matches, back[:, None], 0.0), axis=0)
    dcombine = dcombine.reshape(tok_rows, top_count)

    rank = lax.axis_index("y").reshape(1)
    update = last_step(rank, rows_t, packs, ups)
    return (update, dcombine)


def build(mesh, plane):
    split_mesh = Mesh(
        mesh.devices.reshape(plane + (mesh.devices.shape[1],)), ("x", "z", "c", "y")
    )
    expert = ("x", "z", "c")
    in_specs = (
        P(expert, "y"),
        P(expert, "y"),
        P(expert, None),
        P(expert, None),
        P(expert, "y", None),
        P(expert, None, "y"),
        P(expert, None, "y"),
    )
    out_specs = (P(expert, "y", None), P(expert, None))
    return jax.shard_map(
        on_device, mesh=split_mesh, in_specs=in_specs, out_specs=out_specs, check_vma=False
    )


def solution(mesh):
    return build(mesh, PLANE)
```

```python
import math

import jax
import jax.numpy as jnp
from jax import lax
from jax.experimental import pallas as pl
from jax.experimental.pallas import tpu as pltpu
from jax.sharding import Mesh
from jax.sharding import PartitionSpec as P

D = 3584
CAP = 6
PLANE = (4, 16, 2)

poly_first = 8.28721201814563
poly_third = -23.595886519098837
poly_fifth = 17.300387312530933

f32, bf16 = jnp.float32, jnp.bfloat16
VMEM = 48 * 1024 * 1024


def dot(a, b, contract):
    return lax.dot_general(a, b, (contract, ((), ())), preferred_element_type=f32)


def block_positions(flat_ids):
    pair_count = flat_ids.shape[0]
    same_id = flat_ids[:, None] == flat_ids[None, :]
    earlier = jnp.arange(pair_count)[None, :] < jnp.arange(pair_count)[:, None]
    return jnp.sum(jnp.logical_and(same_id, earlier), axis=1)


def shift(values, step):
    size = lax.axis_size("y")
    return lax.ppermute(values, "y", [(i, (i + step) % size) for i in range(size)])


def gather_weights(own):
    size, rank = lax.axis_size("y"), lax.axis_index("y")
    own = own.T
    half = own.shape[0] // 2
    before = shift(own, 1)
    after = shift(own, -1)
    far_low = shift(before[:half], 1)
    far_high = shift(after[half:], -1)
    whole = jnp.zeros((size,) + own.shape, own.dtype)
    parts = ((own, 0, 0), (before, -1, 0), (after, 1, 0), (far_low, 2, 0), (far_high, 2, half))
    for part, step, row in parts:
        place = lax.rem(rank + size + step, size)
        whole = lax.dynamic_update_slice(whole, part[None], (place, row, 0))
    return whole


def total(values):
    return jnp.sum(jnp.sum(values, axis=0, keepdims=True), axis=1, keepdims=True)


def swap(values, partner):
    size = lax.axis_size("y")
    return lax.ppermute(values, "y", [(i, partner(i)) for i in range(size)])


def pick_kernel(index_ref, column_ref, out_ref):
    rows, count = index_ref.shape[1], column_ref.shape[1]
    feats = out_ref.shape[-1]
    columns = lax.broadcasted_iota(jnp.int32, (rows, count), 1).astype(f32) + 1.0
    chosen = jnp.where(index_ref[0] == columns, 1.0, 0.0).astype(bf16)
    picked = dot(chosen, column_ref[0], ((1,), (0,)))
    out_ref[...] = picked.reshape(out_ref.shape).astype(bf16)


def pick_rows(index, column, near, part, by_quarter, name):
    quarters, rows, _ = index.shape
    feats = column.shape[2] // 2
    piece = rows // near
    if by_quarter:
        block, place = (1, near, piece, feats), (lambda q: (q, 0, 0, 0))
        shape = (quarters, near, piece, feats)
    else:
        block, place = (near, 1, piece, feats), (lambda q: (0, q, 0, 0))
        shape = (near, quarters, piece, feats)
    return pl.pallas_call(
        pick_kernel,
        grid=(quarters,),
        in_specs=[
            pl.BlockSpec((1, rows, 1), lambda q: (q, 0, 0)),
            pl.BlockSpec((1, column.shape[1], feats), lambda q: (q, 0, part)),
        ],
        out_specs=pl.BlockSpec(block, place),
        out_shape=jax.ShapeDtypeStruct(shape, bf16),
        compiler_params=pltpu.CompilerParams(vmem_limit_bytes=VMEM),
        name=name,
    )(index, column)


def inner_kernel(recv_ref, rows_t_ref, low_ref, high_ref, rows_ref):
    near, quarters, piece, feats = recv_ref.shape
    own = near * piece
    for q in range(quarters):
        rows_ref[q * own : (q + 1) * own] = (
            recv_ref[:, q].astype(f32).reshape(own, feats).astype(bf16)
        )
    half = quarters * own // 2
    top, end = rows_ref[:half], rows_ref[half:]
    low_ref[:half] = dot(top, top, ((1,), (1,))).astype(bf16)
    cross = dot(top, end, ((1,), (1,))).astype(bf16)
    low_ref[half:] = cross[: half // 2]
    high_ref[: half // 2] = cross[half // 2 :]
    high_ref[half // 2 :] = dot(end, end, ((1,), (1,))).astype(bf16)
    rows_t_ref[...] = rows_ref[...].T


def inner_products(recv):
    near, quarters, piece, feats = recv.shape
    slots = near * quarters * piece
    half = slots // 2
    pack = jax.ShapeDtypeStruct((half + half // 2, half), bf16)
    return pl.pallas_call(
        inner_kernel,
        out_shape=[jax.ShapeDtypeStruct((feats, slots), bf16), pack, pack],
        scratch_shapes=[pltpu.VMEM((slots, feats), bf16)],
        compiler_params=pltpu.CompilerParams(vmem_limit_bytes=VMEM),
        name="inner_products",
    )(recv)


def hidden_kernel(
    grads_ref, matrix_ref, saved_ref, weight_ref, low_a, low_b, high_a, high_b,
    up_ref, west_ref, east_ref, dw_ref, rows_ref,
):
    parts, rows, feats = grads_ref.shape
    width = matrix_ref.shape[2]
    hidden_all = up_ref.shape[1]
    half = low_a.shape[1]

    @pl.when(pl.program_id(0) == 0)
    def _():
        for part in range(parts):
            rows_ref[:, part * feats : (part + 1) * feats] = grads_ref[part]
        for one, two, out in ((low_a, low_b, west_ref), (high_a, high_b, east_ref)):
            for i in range(3):
                piece = one[i * rows : (i + 1) * rows].astype(f32)
                piece = piece + two[i * rows : (i + 1) * rows].astype(f32)
                first = hidden_all + i * half
                out[:, first : first + half] = piece.astype(bf16)

    hidden = dot(rows_ref[...], matrix_ref[0], ((1,), (0,)))
    gate = saved_ref[0, :, :width].astype(f32)
    up = saved_ref[0, :, width:].astype(f32)
    act = gate / (1.0 + jnp.exp(-gate))
    scaled = hidden * act
    up_grad = (weight_ref[...] * scaled).astype(bf16)
    place = pl.ds(pl.multiple_of(pl.program_id(0) * width, width), width)
    up_ref[:, place] = up_grad
    west_ref[:, place] = up_grad
    east_ref[:, place] = up_grad
    share = jnp.sum(scaled * up, axis=1, keepdims=True)

    @pl.when(pl.program_id(0) == 0)
    def _():
        dw_ref[...] = share

    @pl.when(pl.program_id(0) != 0)
    def _():
        dw_ref[...] += share


def hidden_step(grads, matrix, saved, weight, sums):
    parts, rows, feats = grads.shape
    blocks, depth, width = matrix.shape
    half = sums[0].shape[1]
    packed = jax.ShapeDtypeStruct((rows, blocks * width + 3 * half), bf16)
    outs = [
        jax.ShapeDtypeStruct((rows, blocks * width), bf16),
        packed,
        packed,
        jax.ShapeDtypeStruct((rows, 1), f32),
    ]
    return pl.pallas_call(
        hidden_kernel,
        grid=(blocks,),
        in_specs=[
            pl.BlockSpec((parts, rows, feats), lambda j: (0, 0, 0)),
            pl.BlockSpec((1, depth, width), lambda j: (j, 0, 0)),
            pl.BlockSpec((1, rows, 2 * width), lambda j: (j, 0, 0)),
            pl.BlockSpec((rows, 1), lambda j: (0, 0)),
        ]
        + [pl.BlockSpec(part.shape, lambda j: (0, 0)) for part in sums],
        out_specs=[pl.BlockSpec(out.shape, lambda j: (0, 0)) for out in outs],
        out_shape=outs,
        scratch_shapes=[pltpu.VMEM((rows, depth), bf16)],
        compiler_params=pltpu.CompilerParams(vmem_limit_bytes=VMEM),
        name="hidden_step",
    )(grads, matrix, saved, weight, *sums)


def last_kernel(
    rank_ref, rows_t_ref, west_a, west_b, east_a, east_b, far_ref, out_ref,
    up_ref, inner_ref, carried_ref, gram_ref, square_ref, poly_ref, start_ref,
):
    rank = rank_ref[0]
    own = far_ref.shape[0]
    slots, hidden = up_ref.shape
    feats = rows_t_ref.shape[0]
    half = slots // 2
    near = rank + 1 - 2 * lax.rem(rank, 2)
    owners = ((rank, west_a), (3 - rank, west_b), (near, east_b), (3 - near, far_ref))
    for owner, part in owners:
        up_ref[pl.ds(pl.multiple_of(owner * own, own), own)] = part[:, :hidden]

    def summed(one, two, i):
        lanes = slice(hidden + i * half, hidden + (i + 1) * half)
        return one[:, lanes].astype(f32) + two[:, lanes].astype(f32)

    low = [summed(west_a, west_b, i) for i in range(3)]
    high = [summed(east_a, east_b, i) for i in range(3)]
    cross = jnp.concatenate([low[2], high[0]], axis=0)
    for i in range(2):
        inner_ref[i * own : (i + 1) * own, :half] = low[i].astype(bf16)
        inner_ref[half + i * own : half + (i + 1) * own, half:] = high[1 + i].astype(bf16)
    inner_ref[:half, half:] = cross.astype(bf16)
    inner_ref[half:, :half] = cross.T.astype(bf16)
    norm = jnp.zeros((1, 1), f32)
    step = slots // 3
    for i in range(0, slots, step):
        carried = dot(inner_ref[i : i + step], up_ref[...], ((1,), (0,)))
        norm = norm + total(carried * up_ref[i : i + step].astype(f32))
        carried_ref[i : i + step] = carried.astype(bf16)
    scale = 1.0 / (1.01 * jnp.sqrt(jnp.maximum(norm, 0.0)) + 1e-07)
    step = hidden // 4
    for i in range(0, hidden, step):
        gram = dot(up_ref[:, i : i + step], carried_ref[...], ((0,), (0,)))
        gram_ref[i : i + step] = (gram * scale * scale).astype(bf16)
    quartic = jnp.zeros((1, 1), f32)
    for i in range(0, hidden, step):
        square = dot(gram_ref[i : i + step], gram_ref[...], ((1,), (0,)))
        quartic = quartic + total(square * square)
        square_ref[i : i + step] = square
    rows = feats // 4
    for i in range(0, feats, rows):
        gradient = dot(rows_t_ref[i : i + rows], up_ref[...], ((1,), (0,)))
        start_ref[i : i + rows] = (gradient * scale).astype(bf16)
    bound = jnp.sqrt(jnp.sqrt(quartic)) + 1e-06
    first_scale = poly_third / bound
    second_scale = poly_fifth / (bound * bound)
    for i in range(0, hidden, step):
        poly_ref[i : i + step] = (
            first_scale * gram_ref[i : i + step].astype(f32)
            + second_scale * square_ref[i : i + step]
        ).astype(bf16)
    for i in range(0, feats, rows):
        start = start_ref[i : i + rows]
        mixed = dot(start, poly_ref[...], ((1,), (0,)))
        out_ref[0, i : i + rows] = (
            math.sqrt(D) * (poly_first * start.astype(f32) + mixed)
        ).astype(bf16)


def last_step(rank, rows_t, parts):
    feats, slots = rows_t.shape
    hidden = parts[-1].shape[1]
    vmem = pl.BlockSpec(memory_space=pltpu.VMEM)
    return pl.pallas_call(
        last_kernel,
        in_specs=[pl.BlockSpec(memory_space=pltpu.SMEM)] + [vmem] * 6,
        out_specs=vmem,
        out_shape=jax.ShapeDtypeStruct((1, feats, hidden), bf16),
        scratch_shapes=[
            pltpu.VMEM((slots, hidden), bf16),
            pltpu.VMEM((slots, slots), bf16),
            pltpu.VMEM((slots, hidden), bf16),
            pltpu.VMEM((hidden, hidden), bf16),
            pltpu.VMEM((hidden, hidden), f32),
            pltpu.VMEM((hidden, hidden), bf16),
            pltpu.VMEM((feats, hidden), bf16),
        ],
        compiler_params=pltpu.CompilerParams(vmem_limit_bytes=VMEM),
        name="last_step",
    )(rank, rows_t, *parts)


def on_device(tokens_in, out_grad, expert_ids, combine, down_weight, gate_saved, up_saved):
    nx, nz, nc = (lax.axis_size(name) for name in ("x", "z", "c"))
    ny = lax.axis_size("y")
    experts = nx * nz * nc
    near = nx * nc
    zl = nz // ny
    slots = experts * CAP
    own_slots = slots // ny
    tok_rows, top_count = expert_ids.shape
    feats = tokens_in.shape[1]
    hidden_part = gate_saved.shape[2]

    column = lax.all_gather(
        jnp.concatenate([tokens_in, out_grad], axis=1), "z", axis=0, tiled=True
    )
    matrix = gather_weights(down_weight[0])

    flat_ids = expert_ids.reshape(-1)
    position = block_positions(flat_ids)
    is_live = flat_ids < experts
    ez = (flat_ids // nc) % nz
    exc = (flat_ids // (nc * nz)) * nc + flat_ids % nc
    target = jnp.where(is_live, (ez * near + exc) * CAP + position, -1)
    matches = target[None, :] == jnp.arange(slots, dtype=jnp.int32)[:, None]
    token_of = (jnp.arange(tok_rows * top_count, dtype=jnp.int32) // top_count).astype(f32) + 1.0
    index_send = jnp.sum(jnp.where(matches, token_of[None, :], 0.0), axis=1)
    weight_send = jnp.sum(
        jnp.where(matches, combine.astype(f32).reshape(1, -1), 0.0), axis=1
    )
    routes = lax.all_to_all(
        jnp.stack([index_send.reshape(nz, near * CAP), weight_send.reshape(nz, near * CAP)], 1),
        "z", 0, 0, tiled=True,
    )
    routes = routes.reshape(nz, 2, near, CAP)
    start = (jnp.arange(nz, dtype=jnp.int32) % zl * tok_rows).astype(f32)[:, None, None]
    index = jnp.where(routes[:, 0] > 0.0, routes[:, 0] + start, 0.0)
    index = index.reshape(ny, zl, near, CAP).transpose(0, 2, 1, 3).reshape(ny, own_slots, 1)
    weight_order = routes[:, 1].reshape(ny, zl, near, CAP).transpose(0, 2, 1, 3)
    weight = lax.all_to_all(
        weight_order.reshape(ny * near, zl * CAP), ("y", "x", "c"), 0, 0, tiled=True
    )
    weight = weight.reshape(ny, own_slots)[0][:, None]

    row = jnp.arange(slots, dtype=jnp.int32)
    rest = row // CAP
    block = rest % zl
    rest = rest // zl
    row_c = rest % nc
    rest = rest // nc
    row_x = rest % nx
    row_q = rest // nx
    source = ((row_x * nz + row_q * zl + block) * nc + row_c) * CAP + row % CAP
    order = (source[:, None] == row[None, :]).astype(bf16)
    saved = jnp.concatenate([gate_saved[0], up_saved[0]], axis=1)
    saved = dot(order, saved, ((1,), (0,))).astype(bf16)
    saved = lax.all_to_all(
        saved.reshape(ny, own_slots, 2 * hidden_part), "y", 0, 0, tiled=True
    )

    column, matrix, saved, weight = lax.optimization_barrier((column, matrix, saved, weight))
    column = column.reshape(ny, zl * tok_rows, 2 * feats)
    token_send = pick_rows(index, column, near, 0, False, "pick_tokens")
    grad_send = pick_rows(index, column, near, 1, True, "pick_grads")
    rows = lax.all_to_all(
        token_send.reshape(near, nz * CAP, feats), ("x", "c"), 0, 0, tiled=True
    ).reshape(near, ny, zl * CAP, feats)
    rows_t, low, high = inner_products(rows)
    beside, across = (lambda i: i ^ 1), (lambda i: ny - 1 - i)
    low_near, high_near = swap(low, beside), swap(high, across)

    grad_send, _ = lax.optimization_barrier((grad_send, rows))
    grads = lax.all_to_all(
        grad_send.reshape(ny * near, zl * CAP, feats), ("y", "x", "c"), 0, 0, tiled=True
    ).reshape(ny, own_slots, feats)
    up_own, west, east, slot_dw = hidden_step(
        grads, matrix, saved, weight, (low, low_near, high, high_near)
    )
    parts = (west, swap(west, across), east, swap(east, beside), shift(up_own, 2))

    back = jnp.broadcast_to(slot_dw.reshape(1, near, zl * CAP), (ny, near, zl * CAP))
    back = lax.all_to_all(
        back.reshape(ny * near, zl * CAP), ("y", "x", "c"), 0, 0, tiled=True
    )
    back = back.reshape(ny, near, zl, CAP).transpose(0, 2, 1, 3).reshape(nz, near, CAP)
    back = jnp.pad(back, ((0, 0), (0, 0), (0, 128 - CAP)))
    back = lax.all_to_all(back, "z", 0, 0, tiled=True)

    rank = lax.axis_index("y").reshape(1)
    update = last_step(rank, rows_t, parts)
    back, update = lax.optimization_barrier((back, update))
    back = back[:, :, :CAP].reshape(-1)
    dcombine = jnp.sum(jnp.where(matches, back[:, None], 0.0), axis=0)
    dcombine = dcombine.reshape(tok_rows, top_count)
    return (update, dcombine)


def build(mesh, plane):
    split_mesh = Mesh(
        mesh.devices.reshape(plane + (mesh.devices.shape[1],)), ("x", "z", "c", "y")
    )
    expert = ("x", "z", "c")
    in_specs = (
        P(expert, "y"),
        P(expert, "y"),
        P(expert, None),
        P(expert, None),
        P(expert, "y", None),
        P(expert, None, "y"),
        P(expert, None, "y"),
    )
    out_specs = (P(expert, "y", None), P(expert, None))
    return jax.shard_map(
        on_device, mesh=split_mesh, in_specs=in_specs, out_specs=out_specs, check_vma=False
    )


def solution(mesh):
    return build(mesh, PLANE)
```

```python
import math

import jax
import jax.numpy as jnp
from jax import lax
from jax.experimental import pallas as pl
from jax.experimental.pallas import tpu as pltpu
from jax.sharding import Mesh
from jax.sharding import PartitionSpec as P

D = 3584
CAP = 6
PLANE = (4, 16, 2)

poly_first = 8.28721201814563
poly_third = -23.595886519098837
poly_fifth = 17.300387312530933

f32, bf16 = jnp.float32, jnp.bfloat16
VMEM = 48 * 1024 * 1024


def dot(a, b, contract):
    return lax.dot_general(a, b, (contract, ((), ())), preferred_element_type=f32)


def block_positions(flat_ids):
    pair_count = flat_ids.shape[0]
    same_id = flat_ids[:, None] == flat_ids[None, :]
    earlier = jnp.arange(pair_count)[None, :] < jnp.arange(pair_count)[:, None]
    return jnp.sum(jnp.logical_and(same_id, earlier), axis=1)


def shift(values, step):
    size = lax.axis_size("y")
    return lax.ppermute(values, "y", [(i, (i + step) % size) for i in range(size)])


def gather_weights(own):
    size, rank = lax.axis_size("y"), lax.axis_index("y")
    own = own.T
    half = own.shape[0] // 2
    before = shift(own, 1)
    after = shift(own, -1)
    far_low = shift(before[:half], 1)
    far_high = shift(after[half:], -1)
    whole = jnp.zeros((size,) + own.shape, own.dtype)
    parts = ((own, 0, 0), (before, -1, 0), (after, 1, 0), (far_low, 2, 0), (far_high, 2, half))
    for part, step, row in parts:
        place = lax.rem(rank + size + step, size)
        whole = lax.dynamic_update_slice(whole, part[None], (place, row, 0))
    return whole


def total(values):
    return jnp.sum(jnp.sum(values, axis=0, keepdims=True), axis=1, keepdims=True)


def swap(values, partner):
    size = lax.axis_size("y")
    return lax.ppermute(values, "y", [(i, partner(i)) for i in range(size)])


def pick_kernel(index_ref, column_ref, out_ref):
    rows, count = index_ref.shape[1], column_ref.shape[1]
    feats = out_ref.shape[-1]
    columns = lax.broadcasted_iota(jnp.int32, (rows, count), 1).astype(f32) + 1.0
    chosen = jnp.where(index_ref[0] == columns, 1.0, 0.0).astype(bf16)
    picked = dot(chosen, column_ref[0], ((1,), (0,)))
    out_ref[...] = picked.reshape(out_ref.shape).astype(bf16)


def pick_rows(index, column, near, part, by_quarter, name):
    quarters, rows, _ = index.shape
    feats = column.shape[2] // 2
    piece = rows // near
    if by_quarter:
        block, place = (1, near, piece, feats), (lambda q: (q, 0, 0, 0))
        shape = (quarters, near, piece, feats)
    else:
        block, place = (near, 1, piece, feats), (lambda q: (0, q, 0, 0))
        shape = (near, quarters, piece, feats)
    return pl.pallas_call(
        pick_kernel,
        grid=(quarters,),
        in_specs=[
            pl.BlockSpec((1, rows, 1), lambda q: (q, 0, 0)),
            pl.BlockSpec((1, column.shape[1], feats), lambda q: (q, 0, part)),
        ],
        out_specs=pl.BlockSpec(block, place),
        out_shape=jax.ShapeDtypeStruct(shape, bf16),
        compiler_params=pltpu.CompilerParams(vmem_limit_bytes=VMEM),
        name=name,
    )(index, column)


def inner_kernel(recv_ref, rows_t_ref, low_ref, high_ref, rows_ref):
    near, quarters, piece, feats = recv_ref.shape
    own = near * piece
    for q in range(quarters):
        rows_ref[q * own : (q + 1) * own] = (
            recv_ref[:, q].astype(f32).reshape(own, feats).astype(bf16)
        )
    half = quarters * own // 2
    top, end = rows_ref[:half], rows_ref[half:]
    low_ref[:half] = dot(top, top, ((1,), (1,))).astype(bf16)
    cross = dot(top, end, ((1,), (1,))).astype(bf16)
    low_ref[half:] = cross[: half // 2]
    high_ref[: half // 2] = cross[half // 2 :]
    high_ref[half // 2 :] = dot(end, end, ((1,), (1,))).astype(bf16)
    rows_t_ref[...] = rows_ref[...].T


def inner_products(recv):
    near, quarters, piece, feats = recv.shape
    slots = near * quarters * piece
    half = slots // 2
    pack = jax.ShapeDtypeStruct((half + half // 2, half), bf16)
    return pl.pallas_call(
        inner_kernel,
        out_shape=[jax.ShapeDtypeStruct((feats, slots), bf16), pack, pack],
        scratch_shapes=[pltpu.VMEM((slots, feats), bf16)],
        compiler_params=pltpu.CompilerParams(vmem_limit_bytes=VMEM),
        name="inner_products",
    )(recv)


def hidden_kernel(grads_ref, matrix_ref, saved_ref, weight_ref, up_ref, dw_ref, hidden_ref):
    blocks, depth, width = matrix_ref.shape
    grads = jnp.concatenate([grads_ref[i] for i in range(grads_ref.shape[0])], axis=1)
    matrix = jnp.concatenate([matrix_ref[j] for j in range(blocks)], axis=1)
    share = dot(grads, matrix, ((1,), (0,)))

    @pl.when(pl.program_id(0) == 0)
    def _():
        hidden_ref[...] = share

    @pl.when(pl.program_id(0) == pl.num_programs(0) - 1)
    def _():
        dw = jnp.zeros((grads.shape[0], 1), f32)
        for j in range(blocks):
            lanes = slice(j * width, (j + 1) * width)
            gate = saved_ref[j, :, :width].astype(f32)
            up = saved_ref[j, :, width:].astype(f32)
            act = gate / (1.0 + jnp.exp(-gate))
            scaled = (hidden_ref[:, lanes] + share[:, lanes]) * act
            up_ref[:, lanes] = (weight_ref[...] * scaled).astype(bf16)
            dw = dw + jnp.sum(scaled * up, axis=1, keepdims=True)
        dw_ref[...] = dw


def hidden_step(grads, matrix, saved, weight):
    parts, rows, feats = grads.shape
    blocks, depth, width = matrix.shape
    outs = [
        jax.ShapeDtypeStruct((rows, blocks * width), bf16),
        jax.ShapeDtypeStruct((rows, 1), f32),
    ]
    return pl.pallas_call(
        hidden_kernel,
        grid=(2,),
        in_specs=[
            pl.BlockSpec((parts // 2, rows, feats), lambda k: (k, 0, 0)),
            pl.BlockSpec((blocks, depth // 2, width), lambda k: (0, k, 0)),
            pl.BlockSpec(saved.shape, lambda k: (0, 0, 0)),
            pl.BlockSpec((rows, 1), lambda k: (0, 0)),
        ],
        out_specs=[pl.BlockSpec(out.shape, lambda k: (0, 0)) for out in outs],
        out_shape=outs,
        scratch_shapes=[pltpu.VMEM((rows, blocks * width), f32)],
        compiler_params=pltpu.CompilerParams(vmem_limit_bytes=VMEM),
        name="hidden_step",
    )(grads, matrix, saved, weight)


def last_kernel(
    rank_ref, rows_t_ref, low_a, low_b, high_a, high_b, own_ref, west_ref, east_ref, far_ref,
    out_ref, up_ref, inner_ref, carried_ref, gram_ref, square_ref, poly_ref, start_ref,
):
    rank = rank_ref[0]
    own = own_ref.shape[0]
    slots, hidden = up_ref.shape
    feats = rows_t_ref.shape[0]
    half = slots // 2
    near = rank + 1 - 2 * lax.rem(rank, 2)
    owners = ((rank, own_ref), (3 - rank, west_ref), (near, east_ref), (3 - near, far_ref))
    for owner, part in owners:
        up_ref[pl.ds(pl.multiple_of(owner * own, own), own)] = part[...]
    low = low_a[...].astype(f32) + low_b[...].astype(f32)
    high = high_a[...].astype(f32) + high_b[...].astype(f32)
    inner_ref[:half, :half] = low[:half].astype(bf16)
    inner_ref[half:, half:] = high[half // 2 :].astype(bf16)
    cross = jnp.concatenate([low[half:], high[: half // 2]], axis=0)
    inner_ref[:half, half:] = cross.astype(bf16)
    inner_ref[half:, :half] = cross.T.astype(bf16)
    norm = jnp.zeros((1, 1), f32)
    step = slots // 3
    for i in range(0, slots, step):
        carried = dot(inner_ref[i : i + step], up_ref[...], ((1,), (0,)))
        norm = norm + total(carried * up_ref[i : i + step].astype(f32))
        carried_ref[i : i + step] = carried.astype(bf16)
    scale = 1.0 / (1.01 * jnp.sqrt(jnp.maximum(norm, 0.0)) + 1e-07)
    step = hidden // 4
    for i in range(0, hidden, step):
        gram = dot(up_ref[:, i : i + step], carried_ref[...], ((0,), (0,)))
        gram_ref[i : i + step] = (gram * scale * scale).astype(bf16)
    quartic = jnp.zeros((1, 1), f32)
    for i in range(0, hidden, step):
        square = dot(gram_ref[i : i + step], gram_ref[...], ((1,), (0,)))
        quartic = quartic + total(square * square)
        square_ref[i : i + step] = square
    rows = feats // 4
    for i in range(0, feats, rows):
        gradient = dot(rows_t_ref[i : i + rows], up_ref[...], ((1,), (0,)))
        start_ref[i : i + rows] = (gradient * scale).astype(bf16)
    bound = jnp.sqrt(jnp.sqrt(quartic)) + 1e-06
    first_scale = poly_third / bound
    second_scale = poly_fifth / (bound * bound)
    for i in range(0, hidden, step):
        poly_ref[i : i + step] = (
            first_scale * gram_ref[i : i + step].astype(f32)
            + second_scale * square_ref[i : i + step]
        ).astype(bf16)
    for i in range(0, feats, rows):
        start = start_ref[i : i + rows]
        mixed = dot(start, poly_ref[...], ((1,), (0,)))
        out_ref[0, i : i + rows] = (
            math.sqrt(D) * (poly_first * start.astype(f32) + mixed)
        ).astype(bf16)


def last_step(rank, rows_t, packs, ups):
    feats, slots = rows_t.shape
    hidden = ups[0].shape[1]
    vmem = pl.BlockSpec(memory_space=pltpu.VMEM)
    return pl.pallas_call(
        last_kernel,
        in_specs=[pl.BlockSpec(memory_space=pltpu.SMEM)] + [vmem] * 9,
        out_specs=vmem,
        out_shape=jax.ShapeDtypeStruct((1, feats, hidden), bf16),
        scratch_shapes=[
            pltpu.VMEM((slots, hidden), bf16),
            pltpu.VMEM((slots, slots), bf16),
            pltpu.VMEM((slots, hidden), bf16),
            pltpu.VMEM((hidden, hidden), bf16),
            pltpu.VMEM((hidden, hidden), f32),
            pltpu.VMEM((hidden, hidden), bf16),
            pltpu.VMEM((feats, hidden), bf16),
        ],
        compiler_params=pltpu.CompilerParams(vmem_limit_bytes=VMEM),
        name="last_step",
    )(rank, rows_t, *packs, *ups)


def on_device(tokens_in, out_grad, expert_ids, combine, down_weight, gate_saved, up_saved):
    nx, nz, nc = (lax.axis_size(name) for name in ("x", "z", "c"))
    ny = lax.axis_size("y")
    experts = nx * nz * nc
    near = nx * nc
    zl = nz // ny
    slots = experts * CAP
    own_slots = slots // ny
    tok_rows, top_count = expert_ids.shape
    feats = tokens_in.shape[1]
    hidden_part = gate_saved.shape[2]

    column = lax.all_gather(
        jnp.concatenate([tokens_in, out_grad], axis=1), "z", axis=0, tiled=True
    )
    matrix = gather_weights(down_weight[0])

    flat_ids = expert_ids.reshape(-1)
    position = block_positions(flat_ids)
    is_live = flat_ids < experts
    ez = (flat_ids // nc) % nz
    exc = (flat_ids // (nc * nz)) * nc + flat_ids % nc
    target = jnp.where(is_live, (ez * near + exc) * CAP + position, -1)
    matches = target[None, :] == jnp.arange(slots, dtype=jnp.int32)[:, None]
    token_of = (jnp.arange(tok_rows * top_count, dtype=jnp.int32) // top_count).astype(f32) + 1.0
    index_send = jnp.sum(jnp.where(matches, token_of[None, :], 0.0), axis=1)
    weight_send = jnp.sum(
        jnp.where(matches, combine.astype(f32).reshape(1, -1), 0.0), axis=1
    )
    routes = lax.all_to_all(
        jnp.stack([index_send.reshape(nz, near * CAP), weight_send.reshape(nz, near * CAP)], 1),
        "z", 0, 0, tiled=True,
    )
    routes = routes.reshape(nz, 2, near, CAP)
    start = (jnp.arange(nz, dtype=jnp.int32) % zl * tok_rows).astype(f32)[:, None, None]
    index = jnp.where(routes[:, 0] > 0.0, routes[:, 0] + start, 0.0)
    index = index.reshape(ny, zl, near, CAP).transpose(0, 2, 1, 3).reshape(ny, own_slots, 1)
    weight_order = routes[:, 1].reshape(ny, zl, near, CAP).transpose(0, 2, 1, 3)
    weight = lax.all_to_all(
        weight_order.reshape(ny * near, zl * CAP), ("y", "x", "c"), 0, 0, tiled=True
    )
    weight = weight.reshape(ny, own_slots)[0][:, None]

    row = jnp.arange(slots, dtype=jnp.int32)
    rest = row // CAP
    block = rest % zl
    rest = rest // zl
    row_c = rest % nc
    rest = rest // nc
    row_x = rest % nx
    row_q = rest // nx
    source = ((row_x * nz + row_q * zl + block) * nc + row_c) * CAP + row % CAP
    order = (source[:, None] == row[None, :]).astype(bf16)
    saved = jnp.concatenate([gate_saved[0], up_saved[0]], axis=1)
    saved = dot(order, saved, ((1,), (0,))).astype(bf16)
    saved = lax.all_to_all(
        saved.reshape(ny, own_slots, 2 * hidden_part), "y", 0, 0, tiled=True
    )

    column, matrix, saved, weight = lax.optimization_barrier((column, matrix, saved, weight))
    column = column.reshape(ny, zl * tok_rows, 2 * feats)
    grad_send = pick_rows(index, column, near, 1, True, "pick_grads")
    token_send = pick_rows(index, column, near, 0, False, "pick_tokens")
    beside, across = (lambda i: i ^ 1), (lambda i: ny - 1 - i)

    grads = lax.all_to_all(
        grad_send.reshape(ny * near, zl * CAP, feats), ("y", "x", "c"), 0, 0, tiled=True
    ).reshape(ny, own_slots, feats)
    token_send, grads = lax.optimization_barrier((token_send, grads))
    up_own, slot_dw = hidden_step(grads, matrix, saved, weight)
    ups = (up_own, swap(up_own, across), swap(up_own, beside), shift(up_own, 2))

    rows = lax.all_to_all(
        token_send.reshape(near, nz * CAP, feats), ("x", "c"), 0, 0, tiled=True
    ).reshape(near, ny, zl * CAP, feats)
    rows, *ups = lax.optimization_barrier((rows, *ups))
    rows_t, low, high = inner_products(rows)
    low = low + swap(low, beside)
    high = high + swap(high, across)
    packs = (low, swap(low, across), high, swap(high, beside))

    back = slot_dw.reshape(near, zl, CAP).transpose(1, 0, 2)
    back = jnp.pad(back, ((0, 0), (0, 0), (0, 128 - CAP)))
    back = lax.dynamic_update_slice(
        jnp.zeros((nz, near, 128), f32), back, (lax.axis_index("y") * zl, 0, 0)
    )
    back, rows_t = lax.optimization_barrier((back, rows_t))
    back = lax.all_to_all(back, "z", 0, 0, tiled=True)[:, :, :CAP]
    back = back.transpose(1, 0, 2).reshape(1, near, nz * CAP)
    back = jnp.broadcast_to(back, (ny, near, nz * CAP)).reshape(ny * near, nz * CAP)
    back = lax.all_to_all(back, ("y", "x", "c"), 0, 0, tiled=True)

    rank = lax.axis_index("y").reshape(1)
    update = last_step(rank, rows_t, packs, ups)
    back, update = lax.optimization_barrier((back, update))
    back = jnp.sum(back.reshape(ny, near, nz, CAP), axis=0).transpose(1, 0, 2).reshape(-1)
    dcombine = jnp.sum(jnp.where(matches, back[:, None], 0.0), axis=0)
    dcombine = dcombine.reshape(tok_rows, top_count)
    return (update, dcombine)


def build(mesh, plane):
    split_mesh = Mesh(
        mesh.devices.reshape(plane + (mesh.devices.shape[1],)), ("x", "z", "c", "y")
    )
    expert = ("x", "z", "c")
    in_specs = (
        P(expert, "y"),
        P(expert, "y"),
        P(expert, None),
        P(expert, None),
        P(expert, "y", None),
        P(expert, None, "y"),
        P(expert, None, "y"),
    )
    out_specs = (P(expert, "y", None), P(expert, None))
    return jax.shard_map(
        on_device, mesh=split_mesh, in_specs=in_specs, out_specs=out_specs, check_vma=False
    )


def solution(mesh):
    return build(mesh, PLANE)
```

```python
import math

import jax
import jax.numpy as jnp
from jax import lax
from jax.experimental import pallas as pl
from jax.experimental.pallas import tpu as pltpu
from jax.sharding import Mesh
from jax.sharding import PartitionSpec as P

D = 3584
CAP = 6
PLANE = (4, 16, 2)

poly_first = 8.28721201814563
poly_third = -23.595886519098837
poly_fifth = 17.300387312530933

f32, bf16 = jnp.float32, jnp.bfloat16
MIB = 1024 * 1024


def dot(a, b, contract):
    return lax.dot_general(a, b, (contract, ((), ())), preferred_element_type=f32)


def block_positions(flat_ids):
    pair_count = flat_ids.shape[0]
    same_id = flat_ids[:, None] == flat_ids[None, :]
    earlier = jnp.arange(pair_count)[None, :] < jnp.arange(pair_count)[:, None]
    return jnp.sum(jnp.logical_and(same_id, earlier), axis=1)


def shift(values, step):
    size = lax.axis_size("y")
    return lax.ppermute(values, "y", [(i, (i + step) % size) for i in range(size)])


def gather_weights(own):
    size, rank = lax.axis_size("y"), lax.axis_index("y")
    own = own.T
    half = own.shape[0] // 2
    before = shift(own, 1)
    after = shift(own, -1)
    far_low = shift(before[:half], 1)
    far_high = shift(after[half:], -1)
    whole = jnp.zeros((size,) + own.shape, own.dtype)
    parts = ((own, 0, 0), (before, -1, 0), (after, 1, 0), (far_low, 2, 0), (far_high, 2, half))
    for part, step, row in parts:
        place = lax.rem(rank + size + step, size)
        whole = lax.dynamic_update_slice(whole, part[None], (place, row, 0))
    return whole


def total(values):
    return jnp.sum(jnp.sum(values, axis=0, keepdims=True), axis=1, keepdims=True)


def swap(values, partner):
    size = lax.axis_size("y")
    return lax.ppermute(values, "y", [(i, partner(i)) for i in range(size)])


def pick_kernel(index_ref, column_ref, out_ref):
    rows, count = index_ref.shape[1], column_ref.shape[1]
    feats = out_ref.shape[-1]
    columns = lax.broadcasted_iota(jnp.int32, (rows, count), 1).astype(f32) + 1.0
    chosen = jnp.where(index_ref[0] == columns, 1.0, 0.0).astype(bf16)
    picked = dot(chosen, column_ref[0], ((1,), (0,)))
    out_ref[...] = picked.reshape(out_ref.shape).astype(bf16)


def pick_rows(index, column, near, part, by_quarter, name):
    quarters, rows, _ = index.shape
    feats = column.shape[2] // 2
    piece = rows // near
    if by_quarter:
        block, place = (1, near, piece, feats), (lambda q: (q, 0, 0, 0))
        shape = (quarters, near, piece, feats)
    else:
        block, place = (near, 1, piece, feats), (lambda q: (0, q, 0, 0))
        shape = (near, quarters, piece, feats)
    return pl.pallas_call(
        pick_kernel,
        grid=(quarters,),
        in_specs=[
            pl.BlockSpec((1, rows, 1), lambda q: (q, 0, 0)),
            pl.BlockSpec((1, column.shape[1], feats), lambda q: (q, 0, part)),
        ],
        out_specs=pl.BlockSpec(block, place),
        out_shape=jax.ShapeDtypeStruct(shape, bf16),
        compiler_params=pltpu.CompilerParams(vmem_limit_bytes=48 * MIB),
        name=name,
    )(index, column)


def inner_kernel(recv_ref, west_ref, east_ref, rows_t_ref, low_ref, high_ref, rows_ref):
    near, quarters, piece, feats = recv_ref.shape
    own, hidden = west_ref.shape
    for q in range(quarters):
        rows_ref[q * own : (q + 1) * own] = (
            recv_ref[:, q].astype(f32).reshape(own, feats).astype(bf16)
        )
    half = 2 * own
    top, end = rows_ref[:half], rows_ref[half:]
    first = dot(top, top, ((1,), (1,))).astype(bf16)
    cross = dot(top, end, ((1,), (1,))).astype(bf16)
    last = dot(end, end, ((1,), (1,))).astype(bf16)
    low_ref[:, :half] = first[:own]
    low_ref[:, half : 2 * half] = first[own:]
    low_ref[:, 2 * half : 3 * half] = cross[:own]
    high_ref[:, :half] = cross[own:]
    high_ref[:, half : 2 * half] = last[:own]
    high_ref[:, 2 * half : 3 * half] = last[own:]
    low_ref[:, 3 * half :] = west_ref[:, : hidden // 2]
    high_ref[:, 3 * half :] = east_ref[:, hidden // 2 :]
    rows_t_ref[...] = rows_ref[...].T


def inner_products(recv, west, east):
    near, quarters, piece, feats = recv.shape
    own, hidden = west.shape
    pack = jax.ShapeDtypeStruct((own, 6 * own + hidden // 2), bf16)
    return pl.pallas_call(
        inner_kernel,
        out_shape=[pltpu.HBM((feats, quarters * own), bf16), pack, pack],
        scratch_shapes=[pltpu.VMEM((quarters * own, feats), bf16)],
        compiler_params=pltpu.CompilerParams(vmem_limit_bytes=20 * MIB),
        name="inner_products",
    )(recv, west, east)


def hidden_kernel(grads_ref, matrix_ref, out_act_ref, dw_act_ref, up_ref, dw_ref, hidden_ref):
    blocks, depth, width = matrix_ref.shape
    grads = jnp.concatenate([grads_ref[i] for i in range(grads_ref.shape[0])], axis=1)
    matrix = jnp.concatenate([matrix_ref[j] for j in range(blocks)], axis=1)
    share = dot(grads, matrix, ((1,), (0,)))

    @pl.when(pl.program_id(0) == 0)
    def _():
        hidden_ref[...] = share

    @pl.when(pl.program_id(0) == pl.num_programs(0) - 1)
    def _():
        dw = jnp.zeros((grads.shape[0], 1), f32)
        for j in range(blocks):
            lanes = slice(j * width, (j + 1) * width)
            hidden = hidden_ref[:, lanes] + share[:, lanes]
            up_ref[:, lanes] = (hidden * out_act_ref[j]).astype(bf16)
            dw = dw + jnp.sum(hidden * dw_act_ref[j], axis=1, keepdims=True)
        dw_ref[...] = dw


def hidden_step(grads, matrix, out_act, dw_act):
    parts, rows, feats = grads.shape
    blocks, depth, width = matrix.shape
    outs = [
        pltpu.HBM((rows, blocks * width), bf16),
        jax.ShapeDtypeStruct((rows, 1), f32),
    ]
    return pl.pallas_call(
        hidden_kernel,
        grid=(2,),
        in_specs=[
            pl.BlockSpec((parts // 2, rows, feats), lambda k: (k, 0, 0)),
            pl.BlockSpec((blocks, depth // 2, width), lambda k: (0, k, 0)),
            pl.BlockSpec(out_act.shape, lambda k: (0, 0, 0)),
            pl.BlockSpec(dw_act.shape, lambda k: (0, 0, 0)),
        ],
        out_specs=[pl.BlockSpec(out.shape, lambda k: (0, 0)) for out in outs],
        out_shape=outs,
        scratch_shapes=[pltpu.VMEM((rows, blocks * width), f32)],
        compiler_params=pltpu.CompilerParams(vmem_limit_bytes=28 * MIB),
        name="hidden_step",
    )(grads, matrix, out_act, dw_act)


def last_kernel(
    rank_ref, rows_t_hbm, own_hbm, low_a, low_b, high_a, high_b, west_ref, east_ref,
    far_low, far_high, out_ref,
    up_ref, inner_ref, carried_ref, gram_ref, square_ref, poly_ref, start_ref, rows_t_ref,
    own_sem, rows_sem,
):
    rank = rank_ref[0]
    own, hidden = west_ref.shape
    feats, slots = rows_t_ref.shape
    half = slots // 2
    near = rank + 1 - 2 * lax.rem(rank, 2)

    def owned(owner):
        return pl.ds(pl.multiple_of(owner * own, own), own)

    own_copy = pltpu.make_async_copy(own_hbm, up_ref.at[owned(rank)], own_sem)
    rows_copy = pltpu.make_async_copy(rows_t_hbm, rows_t_ref, rows_sem)
    own_copy.start()
    rows_copy.start()
    for owner, part in ((3 - rank, west_ref), (near, east_ref)):
        up_ref[owned(owner)] = part[...]
    up_ref[owned(3 - near), : hidden // 2] = far_low[:, 3 * half :]
    up_ref[owned(3 - near), hidden // 2 :] = far_high[:, 3 * half :]

    def summed(one, two, i):
        lanes = slice(i * half, (i + 1) * half)
        return one[:, lanes].astype(f32) + two[:, lanes].astype(f32)

    low = [summed(low_a, low_b, i) for i in range(3)]
    high = [summed(high_a, high_b, i) for i in range(3)]
    cross = jnp.concatenate([low[2], high[0]], axis=0)
    for i in range(2):
        inner_ref[i * own : (i + 1) * own, :half] = low[i].astype(bf16)
        inner_ref[half + i * own : half + (i + 1) * own, half:] = high[1 + i].astype(bf16)
    inner_ref[:half, half:] = cross.astype(bf16)
    inner_ref[half:, :half] = cross.T.astype(bf16)
    own_copy.wait()
    norm = jnp.zeros((1, 1), f32)
    step = slots // 3
    for i in range(0, slots, step):
        carried = dot(inner_ref[i : i + step], up_ref[...], ((1,), (0,)))
        norm = norm + total(carried * up_ref[i : i + step].astype(f32))
        carried_ref[i : i + step] = carried.astype(bf16)
    scale = 1.0 / (1.01 * jnp.sqrt(jnp.maximum(norm, 0.0)) + 1e-07)
    step = hidden // 4
    for i in range(0, hidden, step):
        gram = dot(up_ref[:, i : i + step], carried_ref[...], ((0,), (0,)))
        gram_ref[i : i + step] = (gram * scale * scale).astype(bf16)
    quartic = jnp.zeros((1, 1), f32)
    for i in range(0, hidden, step):
        square = dot(gram_ref[i : i + step], gram_ref[...], ((1,), (0,)))
        quartic = quartic + total(square * square)
        square_ref[i : i + step] = square
    rows = feats // 4
    rows_copy.wait()
    for i in range(0, feats, rows):
        gradient = dot(rows_t_ref[i : i + rows], up_ref[...], ((1,), (0,)))
        start_ref[i : i + rows] = (gradient * scale).astype(bf16)
    bound = jnp.sqrt(jnp.sqrt(quartic)) + 1e-06
    first_scale = poly_third / bound
    second_scale = poly_fifth / (bound * bound)
    for i in range(0, hidden, step):
        poly_ref[i : i + step] = (
            first_scale * gram_ref[i : i + step].astype(f32)
            + second_scale * square_ref[i : i + step]
        ).astype(bf16)
    for i in range(0, feats, rows):
        start = start_ref[i : i + rows]
        mixed = dot(start, poly_ref[...], ((1,), (0,)))
        out_ref[0, i : i + rows] = (
            math.sqrt(D) * (poly_first * start.astype(f32) + mixed)
        ).astype(bf16)


def last_step(rank, rows_t, own, packs, ups):
    feats, slots = rows_t.shape
    hidden = own.shape[1]
    return pl.pallas_call(
        last_kernel,
        in_specs=[pl.BlockSpec(memory_space=pltpu.SMEM)]
        + [pl.BlockSpec(memory_space=pltpu.HBM)] * 2
        + [pl.BlockSpec()] * 8,
        out_shape=jax.ShapeDtypeStruct((1, feats, hidden), bf16),
        scratch_shapes=[
            pltpu.VMEM((slots, hidden), bf16),
            pltpu.VMEM((slots, slots), bf16),
            pltpu.VMEM((slots, hidden), bf16),
            pltpu.VMEM((hidden, hidden), bf16),
            pltpu.VMEM((hidden, hidden), f32),
            pltpu.VMEM((hidden, hidden), bf16),
            pltpu.VMEM((feats, hidden), bf16),
            pltpu.VMEM((feats, slots), bf16),
            pltpu.SemaphoreType.DMA,
            pltpu.SemaphoreType.DMA,
        ],
        compiler_params=pltpu.CompilerParams(vmem_limit_bytes=56 * MIB),
        name="last_step",
    )(rank, rows_t, own, *packs, *ups)


def on_device(tokens_in, out_grad, expert_ids, combine, down_weight, gate_saved, up_saved):
    nx, nz, nc = (lax.axis_size(name) for name in ("x", "z", "c"))
    ny = lax.axis_size("y")
    experts = nx * nz * nc
    near = nx * nc
    zl = nz // ny
    slots = experts * CAP
    own_slots = slots // ny
    tok_rows, top_count = expert_ids.shape
    feats = tokens_in.shape[1]
    hidden_part = gate_saved.shape[2]

    column = lax.all_gather(
        jnp.concatenate([tokens_in, out_grad], axis=1), "z", axis=0, tiled=True
    )
    matrix = gather_weights(down_weight[0])

    flat_ids = expert_ids.reshape(-1)
    position = block_positions(flat_ids)
    is_live = flat_ids < experts
    ez = (flat_ids // nc) % nz
    exc = (flat_ids // (nc * nz)) * nc + flat_ids % nc
    target = jnp.where(is_live, (ez * near + exc) * CAP + position, -1)
    matches = target[None, :] == jnp.arange(slots, dtype=jnp.int32)[:, None]
    token_of = (jnp.arange(tok_rows * top_count, dtype=jnp.int32) // top_count).astype(f32) + 1.0
    index_send = jnp.sum(jnp.where(matches, token_of[None, :], 0.0), axis=1)
    weight_send = jnp.sum(
        jnp.where(matches, combine.astype(f32).reshape(1, -1), 0.0), axis=1
    )
    routes = lax.all_to_all(
        jnp.stack([index_send.reshape(nz, near * CAP), weight_send.reshape(nz, near * CAP)], 1),
        "z", 0, 0, tiled=True,
    )
    routes = routes.reshape(nz, 2, near, CAP)
    start = (jnp.arange(nz, dtype=jnp.int32) % zl * tok_rows).astype(f32)[:, None, None]
    index = jnp.where(routes[:, 0] > 0.0, routes[:, 0] + start, 0.0)
    index = index.reshape(ny, zl, near, CAP).transpose(0, 2, 1, 3).reshape(ny, own_slots, 1)
    weight_order = routes[:, 1].reshape(ny, zl, near, CAP).transpose(0, 2, 1, 3)
    weight = lax.all_to_all(
        weight_order.reshape(ny * near, zl * CAP), ("y", "x", "c"), 0, 0, tiled=True
    )
    weight = weight.reshape(ny, own_slots)[0][:, None]

    row = jnp.arange(slots, dtype=jnp.int32)
    rest = row // CAP
    block = rest % zl
    rest = rest // zl
    row_c = rest % nc
    rest = rest // nc
    row_x = rest % nx
    row_q = rest // nx
    source = ((row_x * nz + row_q * zl + block) * nc + row_c) * CAP + row % CAP
    order = (source[:, None] == row[None, :]).astype(bf16)
    saved = jnp.concatenate([gate_saved[0], up_saved[0]], axis=1)
    saved = dot(order, saved, ((1,), (0,))).astype(bf16)
    saved = lax.all_to_all(
        saved.reshape(ny, own_slots, 2 * hidden_part), "y", 0, 0, tiled=True
    )

    gate, up = saved[:, :, :hidden_part].astype(f32), saved[:, :, hidden_part:].astype(f32)
    act = jax.nn.silu(gate)
    out_act, dw_act = act * weight[None], act * up
    column, matrix, out_act, dw_act = lax.optimization_barrier((column, matrix, out_act, dw_act))
    column = column.reshape(ny, zl * tok_rows, 2 * feats)
    grad_send = pick_rows(index, column, near, 1, True, "pick_grads")
    token_send = pick_rows(index, column, near, 0, False, "pick_tokens")
    beside, across = (lambda i: i ^ 1), (lambda i: ny - 1 - i)

    grads = lax.all_to_all(
        grad_send.reshape(ny * near, zl * CAP, feats), ("y", "x", "c"), 0, 0, tiled=True
    ).reshape(ny, own_slots, feats)
    token_send, grads = lax.optimization_barrier((token_send, grads))
    up_own, slot_dw = hidden_step(grads, matrix, out_act, dw_act)
    west, east = swap(up_own, across), swap(up_own, beside)

    rows = lax.all_to_all(
        token_send.reshape(near, nz * CAP, feats), ("x", "c"), 0, 0, tiled=True
    ).reshape(near, ny, zl * CAP, feats)
    rows_t, low, high = inner_products(rows, west, east)
    size = 6 * own_slots
    low_near, high_near = swap(low, beside), swap(high, across)
    low, high = low[:, :size] + low_near[:, :size], high[:, :size] + high_near[:, :size]
    packs = (low, swap(low, across), high, swap(high, beside))
    ups = (west, east, low_near, high_near)

    back = slot_dw.reshape(near, zl, CAP).transpose(1, 0, 2)
    back = jnp.pad(back, ((0, 0), (0, 0), (0, 128 - CAP)))
    back = lax.dynamic_update_slice(
        jnp.zeros((nz, near, 128), f32), back, (lax.axis_index("y") * zl, 0, 0)
    )
    back, rows_t = lax.optimization_barrier((back, rows_t))
    back = lax.all_to_all(back, "z", 0, 0, tiled=True)[:, :, :CAP]
    back = back.transpose(1, 0, 2).reshape(1, near, nz * CAP)
    back = jnp.broadcast_to(back, (ny, near, nz * CAP)).reshape(ny * near, nz * CAP)
    back = lax.all_to_all(back, ("y", "x", "c"), 0, 0, tiled=True)

    rank = lax.axis_index("y").reshape(1)
    update = last_step(rank, rows_t, up_own, packs, ups)
    back, update = lax.optimization_barrier((back, update))
    back = jnp.sum(back.reshape(ny, near, nz, CAP), axis=0).transpose(1, 0, 2).reshape(-1)
    dcombine = jnp.sum(jnp.where(matches, back[:, None], 0.0), axis=0)
    dcombine = dcombine.reshape(tok_rows, top_count)
    return (update, dcombine)


def build(mesh, plane):
    split_mesh = Mesh(
        mesh.devices.reshape(plane + (mesh.devices.shape[1],)), ("x", "z", "c", "y")
    )
    expert = ("x", "z", "c")
    in_specs = (
        P(expert, "y"),
        P(expert, "y"),
        P(expert, None),
        P(expert, None),
        P(expert, "y", None),
        P(expert, None, "y"),
        P(expert, None, "y"),
    )
    out_specs = (P(expert, "y", None), P(expert, None))
    return jax.shard_map(
        on_device, mesh=split_mesh, in_specs=in_specs, out_specs=out_specs, check_vma=False
    )


def solution(mesh):
    return build(mesh, PLANE)
```

```python
import functools
import math

import jax
import jax.numpy as jnp
from jax import lax
from jax.experimental import pallas as pl
from jax.experimental.pallas import tpu as pltpu
from jax.sharding import Mesh
from jax.sharding import PartitionSpec as P

D = 3584
CAP = 6
PLANE = (4, 16, 2)

poly_first = 8.28721201814563
poly_third = -23.595886519098837
poly_fifth = 17.300387312530933

f32, bf16 = jnp.float32, jnp.bfloat16
MIB = 1024 * 1024


def dot(a, b, contract):
    return lax.dot_general(a, b, (contract, ((), ())), preferred_element_type=f32)


def block_positions(flat_ids):
    pair_count = flat_ids.shape[0]
    same_id = flat_ids[:, None] == flat_ids[None, :]
    earlier = jnp.arange(pair_count)[None, :] < jnp.arange(pair_count)[:, None]
    return jnp.sum(jnp.logical_and(same_id, earlier), axis=1)


def shift(values, step):
    size = lax.axis_size("y")
    return lax.ppermute(values, "y", [(i, (i + step) % size) for i in range(size)])


def gather_weights(own, behind):
    size, rank = lax.axis_size("y"), lax.axis_index("y")
    own = own.T
    half = own.shape[0] // 2
    before = shift(own, 1)
    after = shift(own, -1)
    before, after, behind = lax.optimization_barrier((before, after, behind))
    far_low = shift(before[:half], 1)
    far_high = shift(after[half:], -1)
    whole = jnp.zeros((size,) + own.shape, own.dtype)
    parts = ((own, 0, 0), (before, -1, 0), (after, 1, 0), (far_low, 2, 0), (far_high, 2, half))
    for part, step, row in parts:
        place = lax.rem(rank + size + step, size)
        whole = lax.dynamic_update_slice(whole, part[None], (place, row, 0))
    return whole, behind


def total(values):
    return jnp.sum(jnp.sum(values, axis=0, keepdims=True), axis=1, keepdims=True)


def swap(values, partner):
    size = lax.axis_size("y")
    return lax.ppermute(values, "y", [(i, partner(i)) for i in range(size)])


def pick_kernel(by_quarter, index_ref, column_ref, out_ref):
    quarters, rows, _ = index_ref.shape
    count = column_ref.shape[1]
    piece, feats = out_ref.shape[2:]
    columns = lax.broadcasted_iota(jnp.int32, (rows, count), 1).astype(f32) + 1.0
    for q in range(quarters):
        chosen = jnp.where(index_ref[q] == columns, 1.0, 0.0).astype(bf16)
        picked = dot(chosen, column_ref[q], ((1,), (0,)))
        picked = picked.reshape(rows // piece, piece, feats).astype(bf16)
        if by_quarter:
            out_ref[q] = picked
        else:
            out_ref[:, q] = picked


def pick_rows(index, column, near, part, by_quarter, name):
    quarters, rows, _ = index.shape
    feats = column.shape[2] // 2
    piece = rows // near
    if by_quarter:
        block, place = (2, near, piece, feats), (lambda q: (q, 0, 0, 0))
        shape = (quarters, near, piece, feats)
    else:
        block, place = (near, 2, piece, feats), (lambda q: (0, q, 0, 0))
        shape = (near, quarters, piece, feats)
    return pl.pallas_call(
        functools.partial(pick_kernel, by_quarter),
        grid=(quarters // 2,),
        in_specs=[
            pl.BlockSpec((2, rows, 1), lambda q: (q, 0, 0)),
            pl.BlockSpec((2, column.shape[1], feats), lambda q: (q, 0, part)),
        ],
        out_specs=pl.BlockSpec(block, place),
        out_shape=jax.ShapeDtypeStruct(shape, bf16),
        compiler_params=pltpu.CompilerParams(vmem_limit_bytes=48 * MIB),
        name=name,
    )(index, column)


def inner_kernel(recv_ref, west_ref, east_ref, rows_t_ref, low_ref, high_ref, rows_ref):
    near, quarters, piece, feats = recv_ref.shape
    own, hidden = west_ref.shape
    for q in range(quarters):
        rows_ref[q * own : (q + 1) * own] = (
            recv_ref[:, q].astype(f32).reshape(own, feats).astype(bf16)
        )
    half = 2 * own
    top, end = rows_ref[:half], rows_ref[half:]
    first = dot(top, top, ((1,), (1,))).astype(bf16)
    cross = dot(top, end, ((1,), (1,))).astype(bf16)
    last = dot(end, end, ((1,), (1,))).astype(bf16)
    low_ref[:, :half] = first[:own]
    low_ref[:, half : 2 * half] = first[own:]
    low_ref[:, 2 * half : 3 * half] = cross[:own]
    high_ref[:, :half] = cross[own:]
    high_ref[:, half : 2 * half] = last[:own]
    high_ref[:, 2 * half : 3 * half] = last[own:]
    low_ref[:, 3 * half :] = west_ref[:, : hidden // 2]
    high_ref[:, 3 * half :] = east_ref[:, hidden // 2 :]
    rows_t_ref[...] = rows_ref[...].T


def inner_products(recv, west, east):
    near, quarters, piece, feats = recv.shape
    own, hidden = west.shape
    pack = jax.ShapeDtypeStruct((own, 6 * own + hidden // 2), bf16)
    return pl.pallas_call(
        inner_kernel,
        out_shape=[pltpu.HBM((feats, quarters * own), bf16), pack, pack],
        scratch_shapes=[pltpu.VMEM((quarters * own, feats), bf16)],
        compiler_params=pltpu.CompilerParams(vmem_limit_bytes=20 * MIB),
        name="inner_products",
    )(recv, west, east)


def hidden_kernel(grads_ref, matrix_ref, out_act_ref, dw_act_ref, up_ref, dw_ref, hidden_ref):
    blocks, depth, width = matrix_ref.shape
    grads = jnp.concatenate([grads_ref[i] for i in range(grads_ref.shape[0])], axis=1)
    matrix = jnp.concatenate([matrix_ref[j] for j in range(blocks)], axis=1)
    share = dot(grads, matrix, ((1,), (0,)))

    @pl.when(pl.program_id(0) == 0)
    def _():
        hidden_ref[...] = share

    @pl.when(pl.program_id(0) == pl.num_programs(0) - 1)
    def _():
        dw = jnp.zeros((grads.shape[0], 1), f32)
        for j in range(blocks):
            lanes = slice(j * width, (j + 1) * width)
            hidden = hidden_ref[:, lanes] + share[:, lanes]
            up_ref[:, lanes] = (hidden * out_act_ref[j]).astype(bf16)
            dw = dw + jnp.sum(hidden * dw_act_ref[j], axis=1, keepdims=True)
        dw_ref[...] = dw


def hidden_step(grads, matrix, out_act, dw_act):
    parts, rows, feats = grads.shape
    blocks, depth, width = matrix.shape
    outs = [
        pltpu.HBM((rows, blocks * width), bf16),
        pltpu.HBM((rows, 1), f32),
    ]
    return pl.pallas_call(
        hidden_kernel,
        grid=(2,),
        in_specs=[
            pl.BlockSpec((parts // 2, rows, feats), lambda k: (k, 0, 0)),
            pl.BlockSpec((blocks, depth // 2, width), lambda k: (0, k, 0)),
            pl.BlockSpec(out_act.shape, lambda k: (0, 0, 0)),
            pl.BlockSpec(dw_act.shape, lambda k: (0, 0, 0)),
        ],
        out_specs=[pl.BlockSpec(out.shape, lambda k: (0, 0)) for out in outs],
        out_shape=outs,
        scratch_shapes=[pltpu.VMEM((rows, blocks * width), f32)],
        compiler_params=pltpu.CompilerParams(vmem_limit_bytes=46 * MIB),
        name="hidden_step",
    )(grads, matrix, out_act, dw_act)


def last_kernel(
    rank_ref, rows_t_hbm, own_hbm, low_a, low_b, high_a, high_b, west_hbm, east_hbm,
    far_low, far_high, out_ref,
    up_ref, inner_ref, carried_ref, gram_ref, square_ref, poly_ref, start_ref, rows_t_ref,
    packs_ref, sems,
):
    rank = rank_ref[0]
    own = west_hbm.shape[0]
    slots, hidden = up_ref.shape
    feats = rows_t_ref.shape[0]
    half = slots // 2
    near = rank + 1 - 2 * lax.rem(rank, 2)

    def owned(owner):
        return pl.ds(pl.multiple_of(owner * own, own), own)

    far = owned(3 - near)
    first, second = pl.ds(0, hidden // 2), pl.ds(hidden // 2, hidden // 2)
    riding = pl.ds(3 * half, hidden // 2)
    moves = [
        (low_a, packs_ref.at[0]),
        (low_b, packs_ref.at[1]),
        (high_a, packs_ref.at[2]),
        (high_b, packs_ref.at[3]),
        (own_hbm, up_ref.at[owned(rank)]),
        (west_hbm, up_ref.at[owned(3 - rank)]),
        (east_hbm, up_ref.at[owned(near)]),
        (far_low.at[:, riding], up_ref.at[far, first]),
        (far_high.at[:, riding], up_ref.at[far, second]),
        (rows_t_hbm, rows_t_ref),
    ]
    copies = [
        pltpu.make_async_copy(source, place, sems.at[i])
        for i, (source, place) in enumerate(moves)
    ]
    for copy in copies:
        copy.start()
    for copy in copies[:4]:
        copy.wait()

    def summed(one, i):
        lanes = slice(i * half, (i + 1) * half)
        return packs_ref[one, :, lanes].astype(f32) + packs_ref[one + 1, :, lanes].astype(f32)

    low = [summed(0, i) for i in range(3)]
    high = [summed(2, i) for i in range(3)]
    cross = jnp.concatenate([low[2], high[0]], axis=0)
    for i in range(2):
        inner_ref[i * own : (i + 1) * own, :half] = low[i].astype(bf16)
        inner_ref[half + i * own : half + (i + 1) * own, half:] = high[1 + i].astype(bf16)
    inner_ref[:half, half:] = cross.astype(bf16)
    inner_ref[half:, :half] = cross.T.astype(bf16)
    for copy in copies[4:9]:
        copy.wait()
    norm = jnp.zeros((1, 1), f32)
    step = slots // 3
    for i in range(0, slots, step):
        carried = dot(inner_ref[i : i + step], up_ref[...], ((1,), (0,)))
        norm = norm + total(carried * up_ref[i : i + step].astype(f32))
        carried_ref[i : i + step] = carried.astype(bf16)
    scale = 1.0 / (1.01 * jnp.sqrt(jnp.maximum(norm, 0.0)) + 1e-07)
    step = hidden // 4
    for i in range(0, hidden, step):
        gram = dot(up_ref[:, i : i + step], carried_ref[...], ((0,), (0,)))
        gram_ref[i : i + step] = (gram * scale * scale).astype(bf16)
    quartic = jnp.zeros((1, 1), f32)
    for i in range(0, hidden, step):
        square = dot(gram_ref[i : i + step], gram_ref[...], ((1,), (0,)))
        quartic = quartic + total(square * square)
        square_ref[i : i + step] = square
    rows = feats // 4
    copies[9].wait()
    for i in range(0, feats, rows):
        gradient = dot(rows_t_ref[i : i + rows], up_ref[...], ((1,), (0,)))
        start_ref[i : i + rows] = (gradient * scale).astype(bf16)
    bound = jnp.sqrt(jnp.sqrt(quartic)) + 1e-06
    first_scale = poly_third / bound
    second_scale = poly_fifth / (bound * bound)
    for i in range(0, hidden, step):
        poly_ref[i : i + step] = (
            first_scale * gram_ref[i : i + step].astype(f32)
            + second_scale * square_ref[i : i + step]
        ).astype(bf16)
    for i in range(0, feats, rows):
        start = start_ref[i : i + rows]
        mixed = dot(start, poly_ref[...], ((1,), (0,)))
        out_ref[0, i : i + rows] = (
            math.sqrt(D) * (poly_first * start.astype(f32) + mixed)
        ).astype(bf16)


def last_step(rank, rows_t, own, packs, ups):
    feats, slots = rows_t.shape
    hidden = own.shape[1]
    return pl.pallas_call(
        last_kernel,
        in_specs=[pl.BlockSpec(memory_space=pltpu.SMEM)]
        + [pl.BlockSpec(memory_space=pltpu.HBM)] * 10,
        out_shape=jax.ShapeDtypeStruct((1, feats, hidden), bf16),
        scratch_shapes=[
            pltpu.VMEM((slots, hidden), bf16),
            pltpu.VMEM((slots, slots), bf16),
            pltpu.VMEM((slots, hidden), bf16),
            pltpu.VMEM((hidden, hidden), bf16),
            pltpu.VMEM((hidden, hidden), f32),
            pltpu.VMEM((hidden, hidden), bf16),
            pltpu.VMEM((feats, hidden), bf16),
            pltpu.VMEM((feats, slots), bf16),
            pltpu.VMEM((4,) + packs[0].shape, bf16),
            pltpu.SemaphoreType.DMA((10,)),
        ],
        compiler_params=pltpu.CompilerParams(vmem_limit_bytes=56 * MIB),
        name="last_step",
    )(rank, rows_t, own, *packs, *ups)


def on_device(tokens_in, out_grad, expert_ids, combine, down_weight, gate_saved, up_saved):
    nx, nz, nc = (lax.axis_size(name) for name in ("x", "z", "c"))
    ny = lax.axis_size("y")
    experts = nx * nz * nc
    near = nx * nc
    zl = nz // ny
    slots = experts * CAP
    own_slots = slots // ny
    tok_rows, top_count = expert_ids.shape
    feats = tokens_in.shape[1]
    hidden_part = gate_saved.shape[2]

    column = lax.all_gather(
        jnp.concatenate([tokens_in, out_grad], axis=1), "z", axis=0, tiled=True
    )

    flat_ids = expert_ids.reshape(-1)
    position = block_positions(flat_ids)
    is_live = flat_ids < experts
    ez = (flat_ids // nc) % nz
    exc = (flat_ids // (nc * nz)) * nc + flat_ids % nc
    target = jnp.where(is_live, (ez * near + exc) * CAP + position, -1)
    matches = target[None, :] == jnp.arange(slots, dtype=jnp.int32)[:, None]
    token_of = (jnp.arange(tok_rows * top_count, dtype=jnp.int32) // top_count).astype(f32) + 1.0
    index_send = jnp.sum(jnp.where(matches, token_of[None, :], 0.0), axis=1)
    weight_send = jnp.sum(
        jnp.where(matches, combine.astype(f32).reshape(1, -1), 0.0), axis=1
    )
    routes = lax.all_to_all(
        jnp.stack([index_send.reshape(nz, near * CAP), weight_send.reshape(nz, near * CAP)], 1),
        "z", 0, 0, tiled=True,
    )
    routes = routes.reshape(nz, 2, near, CAP)
    start = (jnp.arange(nz, dtype=jnp.int32) % zl * tok_rows).astype(f32)[:, None, None]
    index = jnp.where(routes[:, 0] > 0.0, routes[:, 0] + start, 0.0)
    index = index.reshape(ny, zl, near, CAP).transpose(0, 2, 1, 3).reshape(ny, own_slots, 1)
    weight = routes[:, 1].reshape(ny, zl, near, CAP).transpose(0, 2, 1, 3)
    weight = lax.dynamic_index_in_dim(weight, lax.axis_index("y"), 0, keepdims=False)
    weight = lax.all_to_all(weight.reshape(near, zl * CAP), ("x", "c"), 0, 0, tiled=True)
    weight = weight.reshape(own_slots)[:, None]

    row = jnp.arange(slots, dtype=jnp.int32)
    rest = row // CAP
    block = rest % zl
    rest = rest // zl
    row_c = rest % nc
    rest = rest // nc
    row_x = rest % nx
    row_q = rest // nx
    source = ((row_x * nz + row_q * zl + block) * nc + row_c) * CAP + row % CAP
    order = (source[:, None] == row[None, :]).astype(bf16)
    saved = jnp.concatenate([gate_saved[0], up_saved[0]], axis=1)
    saved = dot(order, saved, ((1,), (0,))).astype(bf16)
    matrix, saved = gather_weights(down_weight[0], saved)
    saved = lax.all_to_all(
        saved.reshape(ny, own_slots, 2 * hidden_part), "y", 0, 0, tiled=True
    )

    gate, up = saved[:, :, :hidden_part].astype(f32), saved[:, :, hidden_part:].astype(f32)
    act = jax.nn.silu(gate)
    out_act, dw_act = act * weight[None], act * up
    column, matrix, out_act, dw_act = lax.optimization_barrier((column, matrix, out_act, dw_act))
    column = column.reshape(ny, zl * tok_rows, 2 * feats)
    grad_send = pick_rows(index, column, near, 1, True, "pick_grads")
    token_send = pick_rows(index, column, near, 0, False, "pick_tokens")
    beside, across = (lambda i: i ^ 1), (lambda i: ny - 1 - i)

    grads = lax.all_to_all(
        grad_send.reshape(ny * near, zl * CAP, feats), ("y", "x", "c"), 0, 0, tiled=True
    ).reshape(ny, own_slots, feats)
    token_send, grads = lax.optimization_barrier((token_send, grads))
    up_own, slot_dw = hidden_step(grads, matrix, out_act, dw_act)
    west, east = swap(up_own, across), swap(up_own, beside)

    rows = lax.all_to_all(
        token_send.reshape(near, nz * CAP, feats), ("x", "c"), 0, 0, tiled=True
    ).reshape(near, ny, zl * CAP, feats)
    rows_t, low, high = inner_products(rows, west, east)
    size = 6 * own_slots
    low_near, high_near = swap(low, beside), swap(high, across)
    low, high = low[:, :size] + low_near[:, :size], high[:, :size] + high_near[:, :size]
    packs = (low, swap(low, across), high, swap(high, beside))
    ups = (west, east, low_near, high_near)

    back = slot_dw.reshape(near, zl, CAP).transpose(1, 0, 2)
    back = jnp.pad(back, ((0, 0), (0, 0), (0, 128 - CAP)))
    back = lax.dynamic_update_slice(
        jnp.zeros((nz, near, 128), f32), back, (lax.axis_index("y") * zl, 0, 0)
    )
    back, rows_t = lax.optimization_barrier((back, rows_t))
    back = lax.all_to_all(back, "z", 0, 0, tiled=True)[:, :, :CAP]
    back = back.transpose(1, 0, 2).reshape(1, near, nz * CAP)
    back = jnp.broadcast_to(back, (ny, near, nz * CAP)).reshape(ny * near, nz * CAP)
    back = lax.all_to_all(back, ("y", "x", "c"), 0, 0, tiled=True)

    rank = lax.axis_index("y").reshape(1)
    update = last_step(rank, rows_t, up_own, packs, ups)
    back, update = lax.optimization_barrier((back, update))
    back = jnp.sum(back.reshape(ny, near, nz, CAP), axis=0).transpose(1, 0, 2).reshape(-1)
    dcombine = jnp.sum(jnp.where(matches, back[:, None], 0.0), axis=0)
    dcombine = dcombine.reshape(tok_rows, top_count)
    return (update, dcombine)


def build(mesh, plane):
    split_mesh = Mesh(
        mesh.devices.reshape(plane + (mesh.devices.shape[1],)), ("x", "z", "c", "y")
    )
    expert = ("x", "z", "c")
    in_specs = (
        P(expert, "y"),
        P(expert, "y"),
        P(expert, None),
        P(expert, None),
        P(expert, "y", None),
        P(expert, None, "y"),
        P(expert, None, "y"),
    )
    out_specs = (P(expert, "y", None), P(expert, None))
    return jax.shard_map(
        on_device, mesh=split_mesh, in_specs=in_specs, out_specs=out_specs, check_vma=False
    )


def solution(mesh):
    return build(mesh, PLANE)
```

```python
import functools
import math

import jax
import jax.numpy as jnp
from jax import lax
from jax.experimental import pallas as pl
from jax.experimental.pallas import tpu as pltpu
from jax.sharding import Mesh
from jax.sharding import PartitionSpec as P

D = 3584
CAP = 6
PLANE = (4, 16, 2)

poly_first = 8.28721201814563
poly_third = -23.595886519098837
poly_fifth = 17.300387312530933

f32, bf16 = jnp.float32, jnp.bfloat16
MIB = 1024 * 1024


def dot(a, b, contract):
    return lax.dot_general(a, b, (contract, ((), ())), preferred_element_type=f32)


def block_positions(flat_ids):
    pair_count = flat_ids.shape[0]
    same_id = flat_ids[:, None] == flat_ids[None, :]
    earlier = jnp.arange(pair_count)[None, :] < jnp.arange(pair_count)[:, None]
    return jnp.sum(jnp.logical_and(same_id, earlier), axis=1)


def shift(values, step):
    size = lax.axis_size("y")
    return lax.ppermute(values, "y", [(i, (i + step) % size) for i in range(size)])


def gather_weights(own, behind):
    size, rank = lax.axis_size("y"), lax.axis_index("y")
    own = own.T
    half = own.shape[0] // 2
    before = shift(own, 1)
    after = shift(own, -1)
    before, after, behind = lax.optimization_barrier((before, after, behind))
    far_low = shift(before[:half], 1)
    far_high = shift(after[half:], -1)
    whole = jnp.zeros((size,) + own.shape, own.dtype)
    parts = ((own, 0, 0), (before, -1, 0), (after, 1, 0), (far_low, 2, 0), (far_high, 2, half))
    for part, step, row in parts:
        place = lax.rem(rank + size + step, size)
        whole = lax.dynamic_update_slice(whole, part[None], (place, row, 0))
    return whole, behind


def total(values):
    return jnp.sum(jnp.sum(values, axis=0, keepdims=True), axis=1, keepdims=True)


def swap(values, partner):
    size = lax.axis_size("y")
    return lax.ppermute(values, "y", [(i, partner(i)) for i in range(size)])


def pick_kernel(by_quarter, index_ref, column_ref, out_ref):
    quarters, rows, _ = index_ref.shape
    count = column_ref.shape[1]
    piece, feats = out_ref.shape[2:]
    columns = lax.broadcasted_iota(jnp.int32, (rows, count), 1).astype(f32) + 1.0
    for q in range(quarters):
        chosen = jnp.where(index_ref[q] == columns, 1.0, 0.0).astype(bf16)
        picked = dot(chosen, column_ref[q], ((1,), (0,)))
        picked = picked.reshape(rows // piece, piece, feats).astype(bf16)
        if by_quarter:
            out_ref[q] = picked
        else:
            out_ref[:, q] = picked


def pick_rows(index, column, near, part, by_quarter, name):
    quarters, rows, _ = index.shape
    feats = column.shape[2] // 2
    piece = rows // near
    if by_quarter:
        block, place = (2, near, piece, feats), (lambda q: (q, 0, 0, 0))
        shape = (quarters, near, piece, feats)
    else:
        block, place = (near, 2, piece, feats), (lambda q: (0, q, 0, 0))
        shape = (near, quarters, piece, feats)
    return pl.pallas_call(
        functools.partial(pick_kernel, by_quarter),
        grid=(quarters // 2,),
        in_specs=[
            pl.BlockSpec((2, rows, 1), lambda q: (q, 0, 0)),
            pl.BlockSpec((2, column.shape[1], feats), lambda q: (q, 0, part)),
        ],
        out_specs=pl.BlockSpec(block, place),
        out_shape=jax.ShapeDtypeStruct(shape, bf16),
        compiler_params=pltpu.CompilerParams(vmem_limit_bytes=48 * MIB),
        name=name,
    )(index, column)


TRIANGLE = ((0, 3, 4), (1, 2, 5))


def triangle(which):
    first, places = 0, []
    for i in TRIANGLE[which]:
        places.append((i, first))
        first += 6 - i
    return places, first


def inner_kernel(recv_ref, west_ref, east_ref, rows_t_ref, low_ref, high_ref, rows_ref):
    near, quarters, piece, feats = recv_ref.shape
    own, hidden = west_ref.shape
    for q in range(quarters):
        rows_ref[q * own : (q + 1) * own] = (
            recv_ref[:, q].astype(f32).reshape(own, feats).astype(bf16)
        )
    side = quarters * own // 6
    lanes = hidden // 2
    for which, out, riding in ((0, low_ref, west_ref), (1, high_ref, east_ref)):
        places, blocks = triangle(which)
        for i, first in places:
            part = dot(rows_ref[i * side : (i + 1) * side], rows_ref[i * side :], ((1,), (1,)))
            out[:, first * side : (first + 6 - i) * side] = part.astype(bf16)
        end, base = blocks * side, which * lanes
        out[:, end : end + lanes] = riding[:side, base : base + lanes]
        end += lanes
        for j in range(2):
            spread = riding[side:, base + j * lanes // 2 : base + (j + 1) * lanes // 2]
            out[j * side // 2 : (j + 1) * side // 2, end : end + lanes // 2] = spread
    rows_t_ref[...] = rows_ref[...].T


def inner_products(recv, west, east):
    near, quarters, piece, feats = recv.shape
    own, hidden = west.shape
    side = quarters * own // 6
    packs = [
        jax.ShapeDtypeStruct((side, triangle(i)[1] * side + 3 * hidden // 4), bf16)
        for i in range(2)
    ]
    return pl.pallas_call(
        inner_kernel,
        out_shape=[pltpu.HBM((feats, quarters * own), bf16), *packs],
        scratch_shapes=[pltpu.VMEM((quarters * own, feats), bf16)],
        compiler_params=pltpu.CompilerParams(vmem_limit_bytes=20 * MIB),
        name="inner_products",
    )(recv, west, east)


def hidden_kernel(grads_ref, matrix_ref, out_act_ref, dw_act_ref, up_ref, dw_ref, hidden_ref):
    blocks, depth, width = matrix_ref.shape
    grads = jnp.concatenate([grads_ref[i] for i in range(grads_ref.shape[0])], axis=1)
    matrix = jnp.concatenate([matrix_ref[j] for j in range(blocks)], axis=1)
    share = dot(grads, matrix, ((1,), (0,)))

    @pl.when(pl.program_id(0) == 0)
    def _():
        hidden_ref[...] = share

    @pl.when(pl.program_id(0) == pl.num_programs(0) - 1)
    def _():
        dw = jnp.zeros((grads.shape[0], 1), f32)
        for j in range(blocks):
            lanes = slice(j * width, (j + 1) * width)
            hidden = hidden_ref[:, lanes] + share[:, lanes]
            up_ref[:, lanes] = (hidden * out_act_ref[j]).astype(bf16)
            dw = dw + jnp.sum(hidden * dw_act_ref[j], axis=1, keepdims=True)
        dw_ref[...] = dw


def hidden_step(grads, matrix, out_act, dw_act):
    parts, rows, feats = grads.shape
    blocks, depth, width = matrix.shape
    outs = [
        pltpu.HBM((rows, blocks * width), bf16),
        pltpu.HBM((rows, 1), f32),
    ]
    return pl.pallas_call(
        hidden_kernel,
        grid=(2,),
        in_specs=[
            pl.BlockSpec((parts // 2, rows, feats), lambda k: (k, 0, 0)),
            pl.BlockSpec((blocks, depth // 2, width), lambda k: (0, k, 0)),
            pl.BlockSpec(out_act.shape, lambda k: (0, 0, 0)),
            pl.BlockSpec(dw_act.shape, lambda k: (0, 0, 0)),
        ],
        out_specs=[pl.BlockSpec(out.shape, lambda k: (0, 0)) for out in outs],
        out_shape=outs,
        scratch_shapes=[pltpu.VMEM((rows, blocks * width), f32)],
        compiler_params=pltpu.CompilerParams(vmem_limit_bytes=46 * MIB),
        name="hidden_step",
    )(grads, matrix, out_act, dw_act)


def last_kernel(
    rank_ref, rows_t_hbm, own_hbm, low_a, low_b, high_a, high_b, west_hbm, east_hbm,
    far_low, far_high, out_ref,
    up_ref, inner_ref, carried_ref, gram_ref, square_ref, poly_ref, start_ref, rows_t_ref,
    low_ref, high_ref, sems, up_t_ref,
):
    rank = rank_ref[0]
    own = west_hbm.shape[0]
    slots, hidden = up_ref.shape
    feats = rows_t_ref.shape[0]
    side, lanes = slots // 6, hidden // 2
    near = rank + 1 - 2 * lax.rem(rank, 2)

    def owned(owner, first=0, rows=own):
        return pl.ds(pl.multiple_of(owner * own + first, 16), rows)

    moves = [
        (low_a, low_ref.at[0]),
        (low_b, low_ref.at[1]),
        (high_a, high_ref.at[0]),
        (high_b, high_ref.at[1]),
        (own_hbm, up_ref.at[owned(rank)]),
        (west_hbm, up_ref.at[owned(3 - rank)]),
        (east_hbm, up_ref.at[owned(near)]),
    ]
    for which, source in ((0, far_low), (1, far_high)):
        end, base = triangle(which)[1] * side, which * lanes
        place = up_ref.at[owned(3 - near, 0, side), pl.ds(base, lanes)]
        moves.append((source.at[:, pl.ds(end, lanes)], place))
        end += lanes
        for j in range(2):
            rows = pl.ds(j * side // 2, side // 2)
            place = pl.ds(base + j * lanes // 2, lanes // 2)
            place = up_ref.at[owned(3 - near, side, side // 2), place]
            moves.append((source.at[rows, pl.ds(end, lanes // 2)], place))
    moves.append((rows_t_hbm, rows_t_ref))
    copies = [
        pltpu.make_async_copy(source, place, sems.at[i])
        for i, (source, place) in enumerate(moves)
    ]
    for copy in copies:
        copy.start()
    for copy in copies[:4]:
        copy.wait()
    for which, packs in ((0, low_ref), (1, high_ref)):
        for i, first in triangle(which)[0]:
            at = slice(first * side, (first + 6 - i) * side)
            part = (packs[0, :, at].astype(f32) + packs[1, :, at].astype(f32)).astype(bf16)
            inner_ref[i * side : (i + 1) * side, i * side :] = part
            for j in range(i + 1, 6):
                block = part[:, (j - i) * side : (j - i + 1) * side].T
                inner_ref[j * side : (j + 1) * side, i * side : (i + 1) * side] = block
    for copy in copies[4:13]:
        copy.wait()
    up_t_ref[...] = up_ref[...].T
    norm = jnp.zeros((1, 1), f32)
    step = slots // 2
    for i in range(0, slots, step):
        carried = dot(inner_ref[i : i + step], up_ref[...], ((1,), (0,)))
        norm = norm + total(carried * up_ref[i : i + step].astype(f32))
        carried_ref[i : i + step] = carried.astype(bf16)
    scale = 1.0 / (1.01 * jnp.sqrt(jnp.maximum(norm, 0.0)) + 1e-07)
    step = hidden // 4
    for i in range(0, hidden, step):
        gram = dot(up_t_ref[i : i + step], carried_ref[:, i:], ((1,), (0,)))
        gram = (gram * scale * scale).astype(bf16)
        gram_ref[i : i + step, i:] = gram
        for j in range(i + step, hidden, step):
            gram_ref[j : j + step, i : i + step] = gram[:, j - i : j - i + step].T
    quartic = jnp.zeros((1, 1), f32)
    for i in range(0, hidden, step):
        square = dot(gram_ref[i : i + step], gram_ref[:, i:], ((1,), (0,)))
        quartic = quartic + 2.0 * total(square * square) - total(square[:, :step] * square[:, :step])
        square_ref[i : i + step, i:] = square
    rows = feats // 2
    copies[13].wait()
    for i in range(0, feats, rows):
        gradient = dot(rows_t_ref[i : i + rows], up_ref[...], ((1,), (0,)))
        start_ref[i : i + rows] = (gradient * scale).astype(bf16)
    bound = jnp.sqrt(jnp.sqrt(quartic)) + 1e-06
    first_scale = poly_third / bound
    second_scale = poly_fifth / (bound * bound)
    for i in range(0, hidden, step):
        poly = (
            first_scale * gram_ref[i : i + step, i:].astype(f32)
            + second_scale * square_ref[i : i + step, i:]
        ).astype(bf16)
        poly_ref[i : i + step, i:] = poly
        for j in range(i + step, hidden, step):
            poly_ref[j : j + step, i : i + step] = poly[:, j - i : j - i + step].T
    for i in range(0, feats, rows):
        start = start_ref[i : i + rows]
        mixed = dot(start, poly_ref[...], ((1,), (0,)))
        out_ref[0, i : i + rows] = (
            math.sqrt(D) * (poly_first * start.astype(f32) + mixed)
        ).astype(bf16)


def last_step(rank, rows_t, own, packs, ups):
    feats, slots = rows_t.shape
    hidden = own.shape[1]
    return pl.pallas_call(
        last_kernel,
        in_specs=[pl.BlockSpec(memory_space=pltpu.SMEM)]
        + [pl.BlockSpec(memory_space=pltpu.HBM)] * 10,
        out_shape=jax.ShapeDtypeStruct((1, feats, hidden), bf16),
        scratch_shapes=[
            pltpu.VMEM((slots, hidden), bf16),
            pltpu.VMEM((slots, slots), bf16),
            pltpu.VMEM((slots, hidden), bf16),
            pltpu.VMEM((hidden, hidden), bf16),
            pltpu.VMEM((hidden, hidden), f32),
            pltpu.VMEM((hidden, hidden), bf16),
            pltpu.VMEM((feats, hidden), bf16),
            pltpu.VMEM((feats, slots), bf16),
            pltpu.VMEM((2,) + packs[0].shape, bf16),
            pltpu.VMEM((2,) + packs[2].shape, bf16),
            pltpu.SemaphoreType.DMA((14,)),
            pltpu.VMEM((hidden, slots), bf16),
        ],
        compiler_params=pltpu.CompilerParams(vmem_limit_bytes=56 * MIB),
        name="last_step",
    )(rank, rows_t, own, *packs, *ups)


def on_device(tokens_in, out_grad, expert_ids, combine, down_weight, gate_saved, up_saved):
    nx, nz, nc = (lax.axis_size(name) for name in ("x", "z", "c"))
    ny = lax.axis_size("y")
    experts = nx * nz * nc
    near = nx * nc
    zl = nz // ny
    slots = experts * CAP
    own_slots = slots // ny
    tok_rows, top_count = expert_ids.shape
    feats = tokens_in.shape[1]
    hidden_part = gate_saved.shape[2]

    column = lax.all_gather(
        jnp.concatenate([tokens_in, out_grad], axis=1), "z", axis=0, tiled=True
    )

    flat_ids = expert_ids.reshape(-1)
    position = block_positions(flat_ids)
    is_live = flat_ids < experts
    ez = (flat_ids // nc) % nz
    exc = (flat_ids // (nc * nz)) * nc + flat_ids % nc
    target = jnp.where(is_live, (ez * near + exc) * CAP + position, -1)
    matches = target[None, :] == jnp.arange(slots, dtype=jnp.int32)[:, None]
    token_of = (jnp.arange(tok_rows * top_count, dtype=jnp.int32) // top_count).astype(f32) + 1.0
    index_send = jnp.sum(jnp.where(matches, token_of[None, :], 0.0), axis=1)
    weight_send = jnp.sum(
        jnp.where(matches, combine.astype(f32).reshape(1, -1), 0.0), axis=1
    )
    routes = lax.all_to_all(
        jnp.stack([index_send.reshape(nz, near * CAP), weight_send.reshape(nz, near * CAP)], 1),
        "z", 0, 0, tiled=True,
    )
    routes = routes.reshape(nz, 2, near, CAP)
    start = (jnp.arange(nz, dtype=jnp.int32) % zl * tok_rows).astype(f32)[:, None, None]
    index = jnp.where(routes[:, 0] > 0.0, routes[:, 0] + start, 0.0)
    index = index.reshape(ny, zl, near, CAP).transpose(0, 2, 1, 3).reshape(ny, own_slots, 1)
    weight = routes[:, 1].reshape(ny, zl, near, CAP).transpose(0, 2, 1, 3)
    weight = lax.dynamic_index_in_dim(weight, lax.axis_index("y"), 0, keepdims=False)
    weight = lax.all_to_all(weight.reshape(near, zl * CAP), ("x", "c"), 0, 0, tiled=True)
    weight = weight.reshape(own_slots)[:, None]

    row = jnp.arange(slots, dtype=jnp.int32)
    rest = row // CAP
    block = rest % zl
    rest = rest // zl
    row_c = rest % nc
    rest = rest // nc
    row_x = rest % nx
    row_q = rest // nx
    source = ((row_x * nz + row_q * zl + block) * nc + row_c) * CAP + row % CAP
    order = (source[:, None] == row[None, :]).astype(bf16)
    saved = jnp.concatenate([gate_saved[0], up_saved[0]], axis=1)
    saved = dot(order, saved, ((1,), (0,))).astype(bf16)
    matrix, saved = gather_weights(down_weight[0], saved)
    saved = lax.all_to_all(
        saved.reshape(ny, own_slots, 2 * hidden_part), "y", 0, 0, tiled=True
    )

    gate, up = saved[:, :, :hidden_part].astype(f32), saved[:, :, hidden_part:].astype(f32)
    act = jax.nn.silu(gate)
    out_act, dw_act = act * weight[None], act * up
    column, matrix, out_act, dw_act = lax.optimization_barrier((column, matrix, out_act, dw_act))
    column = column.reshape(ny, zl * tok_rows, 2 * feats)
    grad_send = pick_rows(index, column, near, 1, True, "pick_grads")
    token_send = pick_rows(index, column, near, 0, False, "pick_tokens")
    beside, across = (lambda i: i ^ 1), (lambda i: ny - 1 - i)

    grads = lax.all_to_all(
        grad_send.reshape(ny * near, zl * CAP, feats), ("y", "x", "c"), 0, 0, tiled=True
    ).reshape(ny, own_slots, feats)
    token_send, grads = lax.optimization_barrier((token_send, grads))
    up_own, slot_dw = hidden_step(grads, matrix, out_act, dw_act)
    west, east = swap(up_own, across), swap(up_own, beside)

    rows = lax.all_to_all(
        token_send.reshape(near, nz * CAP, feats), ("x", "c"), 0, 0, tiled=True
    ).reshape(near, ny, zl * CAP, feats)
    rows_t, low, high = inner_products(rows, west, east)
    low_near, high_near = swap(low, beside), swap(high, across)
    low_size, high_size = (triangle(i)[1] * (slots // 6) for i in range(2))
    low = low[:, :low_size] + low_near[:, :low_size]
    high = high[:, :high_size] + high_near[:, :high_size]
    packs = (low, swap(low, across), high, swap(high, beside))
    ups = (west, east, low_near, high_near)

    back = slot_dw.reshape(near, zl, CAP).transpose(1, 0, 2)
    back = jnp.pad(back, ((0, 0), (0, 0), (0, 128 - CAP)))
    back = lax.dynamic_update_slice(
        jnp.zeros((nz, near, 128), f32), back, (lax.axis_index("y") * zl, 0, 0)
    )
    back, rows_t = lax.optimization_barrier((back, rows_t))
    back = lax.all_to_all(back, "z", 0, 0, tiled=True)[:, :, :CAP]
    back = back.transpose(1, 0, 2).reshape(1, near, nz * CAP)
    back = jnp.broadcast_to(back, (ny, near, nz * CAP)).reshape(ny * near, nz * CAP)
    back = lax.all_to_all(back, ("y", "x", "c"), 0, 0, tiled=True)

    rank = lax.axis_index("y").reshape(1)
    update = last_step(rank, rows_t, up_own, packs, ups)
    back, update = lax.optimization_barrier((back, update))
    back = jnp.sum(back.reshape(ny, near, nz, CAP), axis=0).transpose(1, 0, 2).reshape(-1)
    dcombine = jnp.sum(jnp.where(matches, back[:, None], 0.0), axis=0)
    dcombine = dcombine.reshape(tok_rows, top_count)
    return (update, dcombine)


def build(mesh, plane):
    split_mesh = Mesh(
        mesh.devices.reshape(plane + (mesh.devices.shape[1],)), ("x", "z", "c", "y")
    )
    expert = ("x", "z", "c")
    in_specs = (
        P(expert, "y"),
        P(expert, "y"),
        P(expert, None),
        P(expert, None),
        P(expert, "y", None),
        P(expert, None, "y"),
        P(expert, None, "y"),
    )
    out_specs = (P(expert, "y", None), P(expert, None))
    return jax.shard_map(
        on_device, mesh=split_mesh, in_specs=in_specs, out_specs=out_specs, check_vma=False
    )


def solution(mesh):
    return build(mesh, PLANE)
```

```python
import functools
import math

import jax
import jax.numpy as jnp
from jax import lax
from jax.experimental import pallas as pl
from jax.experimental.pallas import tpu as pltpu
from jax.sharding import Mesh
from jax.sharding import PartitionSpec as P

D = 3584
CAP = 6
PLANE = (4, 16, 2)

poly_first = 8.28721201814563
poly_third = -23.595886519098837
poly_fifth = 17.300387312530933

f32, bf16 = jnp.float32, jnp.bfloat16
MIB = 1024 * 1024


def dot(a, b, contract):
    return lax.dot_general(a, b, (contract, ((), ())), preferred_element_type=f32)


def block_positions(flat_ids):
    pair_count = flat_ids.shape[0]
    same_id = flat_ids[:, None] == flat_ids[None, :]
    earlier = jnp.arange(pair_count)[None, :] < jnp.arange(pair_count)[:, None]
    return jnp.sum(jnp.logical_and(same_id, earlier), axis=1)


def shift(values, step):
    size = lax.axis_size("y")
    return lax.ppermute(values, "y", [(i, (i + step) % size) for i in range(size)])


def gather_weights(own, behind):
    size, rank = lax.axis_size("y"), lax.axis_index("y")
    own = own.T
    half = own.shape[0] // 2
    before = shift(own, 1)
    after = shift(own, -1)
    before, after, behind = lax.optimization_barrier((before, after, behind))
    far_low = shift(before[:half], 1)
    far_high = shift(after[half:], -1)
    whole = jnp.zeros((size,) + own.shape, own.dtype)
    parts = ((own, 0, 0), (before, -1, 0), (after, 1, 0), (far_low, 2, 0), (far_high, 2, half))
    for part, step, row in parts:
        place = lax.rem(rank + size + step, size)
        whole = lax.dynamic_update_slice(whole, part[None], (place, row, 0))
    return whole, behind


def total(values):
    return jnp.sum(jnp.sum(values, axis=0, keepdims=True), axis=1, keepdims=True)


def swap(values, partner):
    size = lax.axis_size("y")
    return lax.ppermute(values, "y", [(i, partner(i)) for i in range(size)])


def pick_kernel(by_quarter, index_ref, column_ref, out_ref):
    quarters, rows, _ = index_ref.shape
    count = column_ref.shape[1]
    piece, feats = out_ref.shape[2:]
    columns = lax.broadcasted_iota(jnp.int32, (rows, count), 1).astype(f32) + 1.0
    for q in range(quarters):
        chosen = jnp.where(index_ref[q] == columns, 1.0, 0.0).astype(bf16)
        picked = dot(chosen, column_ref[q], ((1,), (0,)))
        picked = picked.reshape(rows // piece, piece, feats).astype(bf16)
        if by_quarter:
            out_ref[q] = picked
        else:
            out_ref[:, q] = picked


def pick_rows(index, column, near, part, by_quarter, name):
    quarters, rows, _ = index.shape
    feats = column.shape[2] // 2
    piece = rows // near
    if by_quarter:
        block, place = (2, near, piece, feats), (lambda q: (q, 0, 0, 0))
        shape = (quarters, near, piece, feats)
    else:
        block, place = (near, 2, piece, feats), (lambda q: (0, q, 0, 0))
        shape = (near, quarters, piece, feats)
    return pl.pallas_call(
        functools.partial(pick_kernel, by_quarter),
        grid=(quarters // 2,),
        in_specs=[
            pl.BlockSpec((2, rows, 1), lambda q: (q, 0, 0)),
            pl.BlockSpec((2, column.shape[1], feats), lambda q: (q, 0, part)),
        ],
        out_specs=pl.BlockSpec(block, place),
        out_shape=jax.ShapeDtypeStruct(shape, bf16),
        compiler_params=pltpu.CompilerParams(vmem_limit_bytes=48 * MIB),
        name=name,
    )(index, column)


TRIANGLE = ((0, 3, 4), (1, 2, 5))


def triangle(which):
    first, places = 0, []
    for i in TRIANGLE[which]:
        places.append((i, first))
        first += 6 - i
    return places, first


def inner_kernel(recv_ref, west_ref, east_ref, rows_t_ref, low_ref, high_ref, rows_ref):
    near, quarters, piece, feats = recv_ref.shape
    own, hidden = west_ref.shape
    for q in range(quarters):
        rows_ref[q * own : (q + 1) * own] = (
            recv_ref[:, q].astype(f32).reshape(own, feats).astype(bf16)
        )
    side = quarters * own // 6
    lanes = hidden // 2
    for which, out, riding in ((0, low_ref, west_ref), (1, high_ref, east_ref)):
        places, blocks = triangle(which)
        for i, first in places:
            part = dot(rows_ref[i * side : (i + 1) * side], rows_ref[i * side :], ((1,), (1,)))
            out[:, first * side : (first + 6 - i) * side] = part.astype(bf16)
        end, base = blocks * side, which * lanes
        out[:, end : end + lanes] = riding[:side, base : base + lanes]
        end += lanes
        for j in range(2):
            spread = riding[side:, base + j * lanes // 2 : base + (j + 1) * lanes // 2]
            out[j * side // 2 : (j + 1) * side // 2, end : end + lanes // 2] = spread
    rows_t_ref[...] = rows_ref[...].T


def inner_products(recv, west, east):
    near, quarters, piece, feats = recv.shape
    own, hidden = west.shape
    side = quarters * own // 6
    packs = [
        jax.ShapeDtypeStruct((side, triangle(i)[1] * side + 3 * hidden // 4), bf16)
        for i in range(2)
    ]
    return pl.pallas_call(
        inner_kernel,
        out_shape=[pltpu.HBM((feats, quarters * own), bf16), *packs],
        scratch_shapes=[pltpu.VMEM((quarters * own, feats), bf16)],
        compiler_params=pltpu.CompilerParams(vmem_limit_bytes=20 * MIB),
        name="inner_products",
    )(recv, west, east)


def hidden_kernel(grads_ref, matrix_ref, out_act_ref, dw_act_ref, up_ref, dw_ref, hidden_ref):
    blocks, depth, width = matrix_ref.shape
    grads = jnp.concatenate([grads_ref[i] for i in range(grads_ref.shape[0])], axis=1)
    matrix = jnp.concatenate([matrix_ref[j] for j in range(blocks)], axis=1)
    share = dot(grads, matrix, ((1,), (0,)))

    @pl.when(pl.program_id(0) == 0)
    def _():
        hidden_ref[...] = share

    @pl.when(pl.program_id(0) == pl.num_programs(0) - 1)
    def _():
        dw = jnp.zeros((grads.shape[0], 1), f32)
        for j in range(blocks):
            lanes = slice(j * width, (j + 1) * width)
            hidden = hidden_ref[:, lanes] + share[:, lanes]
            up_ref[:, lanes] = (hidden * out_act_ref[j]).astype(bf16)
            dw = dw + jnp.sum(hidden * dw_act_ref[j], axis=1, keepdims=True)
        dw_ref[...] = dw


def hidden_step(grads, matrix, out_act, dw_act):
    parts, rows, feats = grads.shape
    blocks, depth, width = matrix.shape
    outs = [
        pltpu.HBM((rows, blocks * width), bf16),
        pltpu.HBM((rows, 1), f32),
    ]
    return pl.pallas_call(
        hidden_kernel,
        grid=(2,),
        in_specs=[
            pl.BlockSpec((parts // 2, rows, feats), lambda k: (k, 0, 0)),
            pl.BlockSpec((blocks, depth // 2, width), lambda k: (0, k, 0)),
            pl.BlockSpec(out_act.shape, lambda k: (0, 0, 0)),
            pl.BlockSpec(dw_act.shape, lambda k: (0, 0, 0)),
        ],
        out_specs=[pl.BlockSpec(out.shape, lambda k: (0, 0)) for out in outs],
        out_shape=outs,
        scratch_shapes=[pltpu.VMEM((rows, blocks * width), f32)],
        compiler_params=pltpu.CompilerParams(vmem_limit_bytes=53 * MIB),
        name="hidden_step",
    )(grads, matrix, out_act, dw_act)


def last_kernel(
    rank_ref, rows_t_hbm, own_hbm, low_a, low_b, high_a, high_b, west_hbm, east_hbm,
    far_low, far_high, out_ref,
    up_ref, inner_ref, carried_ref, gram_ref, square_ref, poly_ref, start_ref, rows_t_ref,
    low_ref, high_ref, sems, up_t_ref,
):
    rank = rank_ref[0]
    own = west_hbm.shape[0]
    slots, hidden = up_ref.shape
    feats = rows_t_ref.shape[0]
    side, lanes = slots // 6, hidden // 2
    near = rank + 1 - 2 * lax.rem(rank, 2)

    def owned(owner, first=0, rows=own):
        return pl.ds(pl.multiple_of(owner * own + first, 16), rows)

    moves = [
        (low_a, low_ref.at[0]),
        (low_b, low_ref.at[1]),
        (high_a, high_ref.at[0]),
        (high_b, high_ref.at[1]),
        (own_hbm, up_ref.at[owned(rank)]),
        (west_hbm, up_ref.at[owned(3 - rank)]),
        (east_hbm, up_ref.at[owned(near)]),
    ]
    for which, source in ((0, far_low), (1, far_high)):
        end, base = triangle(which)[1] * side, which * lanes
        place = up_ref.at[owned(3 - near, 0, side), pl.ds(base, lanes)]
        moves.append((source.at[:, pl.ds(end, lanes)], place))
        end += lanes
        for j in range(2):
            rows = pl.ds(j * side // 2, side // 2)
            place = pl.ds(base + j * lanes // 2, lanes // 2)
            place = up_ref.at[owned(3 - near, side, side // 2), place]
            moves.append((source.at[rows, pl.ds(end, lanes // 2)], place))
    moves.append((rows_t_hbm, rows_t_ref))
    copies = [
        pltpu.make_async_copy(source, place, sems.at[i])
        for i, (source, place) in enumerate(moves)
    ]
    for copy in copies:
        copy.start()
    for copy in copies[:4]:
        copy.wait()
    for which, packs in ((0, low_ref), (1, high_ref)):
        for i, first in triangle(which)[0]:
            at = slice(first * side, (first + 6 - i) * side)
            part = (packs[0, :, at].astype(f32) + packs[1, :, at].astype(f32)).astype(bf16)
            inner_ref[i * side : (i + 1) * side, i * side :] = part
            for j in range(i + 1, 6):
                block = part[:, (j - i) * side : (j - i + 1) * side].T
                inner_ref[j * side : (j + 1) * side, i * side : (i + 1) * side] = block
    for copy in copies[4:13]:
        copy.wait()
    up_t_ref[...] = up_ref[...].T
    norm = jnp.zeros((1, 1), f32)
    step = slots // 2
    for i in range(0, slots, step):
        carried = dot(inner_ref[i : i + step], up_ref[...], ((1,), (0,)))
        norm = norm + total(carried * up_ref[i : i + step].astype(f32))
        carried_ref[i : i + step] = carried.astype(bf16)
    scale = 1.0 / (1.01 * jnp.sqrt(jnp.maximum(norm, 0.0)) + 1e-07)
    step = hidden // 4
    for i in range(0, hidden, step):
        gram = dot(up_t_ref[i : i + step], carried_ref[:, i:], ((1,), (0,)))
        gram = (gram * scale * scale).astype(bf16)
        gram_ref[i : i + step, i:] = gram
        for j in range(i + step, hidden, step):
            gram_ref[j : j + step, i : i + step] = gram[:, j - i : j - i + step].T
    quartic = jnp.zeros((1, 1), f32)
    for i in range(0, hidden, step):
        square = dot(gram_ref[i : i + step], gram_ref[:, i:], ((1,), (0,)))
        quartic = quartic + 2.0 * total(square * square) - total(square[:, :step] * square[:, :step])
        square_ref[i : i + step, i:] = square
    rows = feats // 2
    copies[13].wait()
    for i in range(0, feats, rows):
        gradient = dot(rows_t_ref[i : i + rows], up_ref[...], ((1,), (0,)))
        start_ref[i : i + rows] = (gradient * scale).astype(bf16)
    bound = jnp.sqrt(jnp.sqrt(quartic)) + 1e-06
    first_scale = poly_third / bound
    second_scale = poly_fifth / (bound * bound)
    for i in range(0, hidden, step):
        poly = (
            first_scale * gram_ref[i : i + step, i:].astype(f32)
            + second_scale * square_ref[i : i + step, i:]
        ).astype(bf16)
        poly_ref[i : i + step, i:] = poly
        for j in range(i + step, hidden, step):
            poly_ref[j : j + step, i : i + step] = poly[:, j - i : j - i + step].T
    for i in range(0, feats, rows):
        start = start_ref[i : i + rows]
        mixed = dot(start, poly_ref[...], ((1,), (0,)))
        out_ref[0, i : i + rows] = (
            math.sqrt(D) * (poly_first * start.astype(f32) + mixed)
        ).astype(bf16)


def last_step(rank, rows_t, own, packs, ups):
    feats, slots = rows_t.shape
    hidden = own.shape[1]
    return pl.pallas_call(
        last_kernel,
        in_specs=[pl.BlockSpec(memory_space=pltpu.SMEM)]
        + [pl.BlockSpec(memory_space=pltpu.HBM)] * 10,
        out_shape=jax.ShapeDtypeStruct((1, feats, hidden), bf16),
        scratch_shapes=[
            pltpu.VMEM((slots, hidden), bf16),
            pltpu.VMEM((slots, slots), bf16),
            pltpu.VMEM((slots, hidden), bf16),
            pltpu.VMEM((hidden, hidden), bf16),
            pltpu.VMEM((hidden, hidden), f32),
            pltpu.VMEM((hidden, hidden), bf16),
            pltpu.VMEM((feats, hidden), bf16),
            pltpu.VMEM((feats, slots), bf16),
            pltpu.VMEM((2,) + packs[0].shape, bf16),
            pltpu.VMEM((2,) + packs[2].shape, bf16),
            pltpu.SemaphoreType.DMA((14,)),
            pltpu.VMEM((hidden, slots), bf16),
        ],
        compiler_params=pltpu.CompilerParams(vmem_limit_bytes=56 * MIB),
        name="last_step",
    )(rank, rows_t, own, *packs, *ups)


def on_device(tokens_in, out_grad, expert_ids, combine, down_weight, gate_saved, up_saved):
    nx, nz, nc = (lax.axis_size(name) for name in ("x", "z", "c"))
    ny = lax.axis_size("y")
    experts = nx * nz * nc
    near = nx * nc
    zl = nz // ny
    slots = experts * CAP
    own_slots = slots // ny
    tok_rows, top_count = expert_ids.shape
    feats = tokens_in.shape[1]
    hidden_part = gate_saved.shape[2]

    column = lax.all_gather(
        jnp.concatenate([tokens_in, out_grad], axis=1), "z", axis=0, tiled=True
    )

    flat_ids = expert_ids.reshape(-1)
    position = block_positions(flat_ids)
    is_live = flat_ids < experts
    ez = (flat_ids // nc) % nz
    exc = (flat_ids // (nc * nz)) * nc + flat_ids % nc
    target = jnp.where(is_live, (ez * near + exc) * CAP + position, -1)
    matches = target[None, :] == jnp.arange(slots, dtype=jnp.int32)[:, None]
    token_of = (jnp.arange(tok_rows * top_count, dtype=jnp.int32) // top_count).astype(f32) + 1.0
    index_send = jnp.sum(jnp.where(matches, token_of[None, :], 0.0), axis=1)
    weight_send = jnp.sum(
        jnp.where(matches, combine.astype(f32).reshape(1, -1), 0.0), axis=1
    )
    routes = lax.all_to_all(
        jnp.stack([index_send.reshape(nz, near * CAP), weight_send.reshape(nz, near * CAP)], 1),
        "z", 0, 0, tiled=True,
    )
    routes = routes.reshape(nz, 2, near, CAP)
    start = (jnp.arange(nz, dtype=jnp.int32) % zl * tok_rows).astype(f32)[:, None, None]
    index = jnp.where(routes[:, 0] > 0.0, routes[:, 0] + start, 0.0)
    index = index.reshape(ny, zl, near, CAP).transpose(0, 2, 1, 3).reshape(ny, own_slots, 1)
    weight = routes[:, 1].reshape(ny, zl, near, CAP).transpose(0, 2, 1, 3)
    weight = lax.dynamic_index_in_dim(weight, lax.axis_index("y"), 0, keepdims=False)
    weight = lax.all_to_all(weight.reshape(near, zl * CAP), ("x", "c"), 0, 0, tiled=True)
    weight = weight.reshape(own_slots)[:, None]

    row = jnp.arange(slots, dtype=jnp.int32)
    rest = row // CAP
    block = rest % zl
    rest = rest // zl
    row_c = rest % nc
    rest = rest // nc
    row_x = rest % nx
    row_q = rest // nx
    source = ((row_x * nz + row_q * zl + block) * nc + row_c) * CAP + row % CAP
    order = (source[:, None] == row[None, :]).astype(bf16)
    saved = jnp.concatenate([gate_saved[0], up_saved[0]], axis=1)
    saved = dot(order, saved, ((1,), (0,))).astype(bf16)
    matrix, saved = gather_weights(down_weight[0], saved)
    saved = lax.all_to_all(
        saved.reshape(ny, own_slots, 2 * hidden_part), "y", 0, 0, tiled=True
    )

    gate, up = saved[:, :, :hidden_part].astype(f32), saved[:, :, hidden_part:].astype(f32)
    act = jax.nn.silu(gate)
    out_act, dw_act = act * weight[None], act * up
    column, matrix, out_act, dw_act = lax.optimization_barrier((column, matrix, out_act, dw_act))
    column = column.reshape(ny, zl * tok_rows, 2 * feats)
    grad_send = pick_rows(index, column, near, 1, True, "pick_grads")
    token_send = pick_rows(index, column, near, 0, False, "pick_tokens")
    beside, across = (lambda i: i ^ 1), (lambda i: ny - 1 - i)

    grads = lax.all_to_all(
        grad_send.reshape(ny * near, zl * CAP, feats), ("y", "x", "c"), 0, 0, tiled=True
    ).reshape(ny, own_slots, feats)
    token_send, grads = lax.optimization_barrier((token_send, grads))
    up_own, slot_dw = hidden_step(grads, matrix, out_act, dw_act)
    west, east = swap(up_own, across), swap(up_own, beside)
    back = slot_dw.reshape(near, zl, CAP).transpose(1, 0, 2)
    back = jnp.pad(back, ((0, 0), (0, 0), (0, 128 - CAP)))
    back = lax.dynamic_update_slice(
        jnp.zeros((nz, near, 128), f32), back, (lax.axis_index("y") * zl, 0, 0)
    )

    rows = lax.all_to_all(
        token_send.reshape(near, nz * CAP, feats), ("x", "c"), 0, 0, tiled=True
    ).reshape(near, ny, zl * CAP, feats)
    west, east, back = lax.optimization_barrier((west, east, back))
    rows_t, low, high = inner_products(rows, west, east)
    low_near, high_near = swap(low, beside), swap(high, across)
    low_size, high_size = (triangle(i)[1] * (slots // 6) for i in range(2))
    low = low[:, :low_size] + low_near[:, :low_size]
    high = high[:, :high_size] + high_near[:, :high_size]
    packs = (low, swap(low, across), high, swap(high, beside))
    ups = (west, east, low_near, high_near)

    back, rows_t = lax.optimization_barrier((back, rows_t))
    back = lax.all_to_all(back, "z", 0, 0, tiled=True)[:, :, :CAP]
    back = back.transpose(1, 0, 2).reshape(1, near, nz * CAP)
    back = jnp.broadcast_to(back, (ny, near, nz * CAP)).reshape(ny * near, nz * CAP)
    back = lax.all_to_all(back, ("y", "x", "c"), 0, 0, tiled=True)

    rank = lax.axis_index("y").reshape(1)
    update = last_step(rank, rows_t, up_own, packs, ups)
    back, update = lax.optimization_barrier((back, update))
    back = jnp.sum(back.reshape(ny, near, nz, CAP), axis=0).transpose(1, 0, 2).reshape(-1)
    dcombine = jnp.sum(jnp.where(matches, back[:, None], 0.0), axis=0)
    dcombine = dcombine.reshape(tok_rows, top_count)
    return (update, dcombine)


def build(mesh, plane):
    split_mesh = Mesh(
        mesh.devices.reshape(plane + (mesh.devices.shape[1],)), ("x", "z", "c", "y")
    )
    expert = ("x", "z", "c")
    in_specs = (
        P(expert, "y"),
        P(expert, "y"),
        P(expert, None),
        P(expert, None),
        P(expert, "y", None),
        P(expert, None, "y"),
        P(expert, None, "y"),
    )
    out_specs = (P(expert, "y", None), P(expert, None))
    return jax.shard_map(
        on_device, mesh=split_mesh, in_specs=in_specs, out_specs=out_specs, check_vma=False
    )


def solution(mesh):
    return build(mesh, PLANE)
```

```python
import functools
import math

import jax
import jax.numpy as jnp
from jax import lax
from jax.experimental import pallas as pl
from jax.experimental.pallas import tpu as pltpu
from jax.sharding import Mesh
from jax.sharding import PartitionSpec as P

D = 3584
CAP = 6
PLANE = (4, 16, 2)

poly_first = 8.28721201814563
poly_third = -23.595886519098837
poly_fifth = 17.300387312530933

f32, bf16 = jnp.float32, jnp.bfloat16
MIB = 1024 * 1024


def dot(a, b, contract):
    return lax.dot_general(a, b, (contract, ((), ())), preferred_element_type=f32)


def block_positions(flat_ids):
    pair_count = flat_ids.shape[0]
    same_id = flat_ids[:, None] == flat_ids[None, :]
    earlier = jnp.arange(pair_count)[None, :] < jnp.arange(pair_count)[:, None]
    return jnp.sum(jnp.logical_and(same_id, earlier), axis=1)


def shift(values, step):
    size = lax.axis_size("y")
    return lax.ppermute(values, "y", [(i, (i + step) % size) for i in range(size)])


def gather_weights(own, behind):
    size, rank = lax.axis_size("y"), lax.axis_index("y")
    own = own.T
    half = own.shape[0] // 2
    before = shift(own, 1)
    after = shift(own, -1)
    before, after, behind = lax.optimization_barrier((before, after, behind))
    far_low = shift(before[:half], 1)
    far_high = shift(after[half:], -1)
    whole = jnp.zeros((size,) + own.shape, own.dtype)
    parts = ((own, 0, 0), (before, -1, 0), (after, 1, 0), (far_low, 2, 0), (far_high, 2, half))
    for part, step, row in parts:
        place = lax.rem(rank + size + step, size)
        whole = lax.dynamic_update_slice(whole, part[None], (place, row, 0))
    return whole, behind


def total(values):
    return jnp.sum(jnp.sum(values, axis=0, keepdims=True), axis=1, keepdims=True)


def swap(values, partner):
    size = lax.axis_size("y")
    return lax.ppermute(values, "y", [(i, partner(i)) for i in range(size)])


def pick_kernel(by_quarter, index_ref, column_ref, out_ref):
    quarters, rows, _ = index_ref.shape
    count = column_ref.shape[1]
    piece, feats = out_ref.shape[2:]
    columns = lax.broadcasted_iota(jnp.int32, (rows, count), 1).astype(f32) + 1.0
    for q in range(quarters):
        chosen = jnp.where(index_ref[q] == columns, 1.0, 0.0).astype(bf16)
        picked = dot(chosen, column_ref[q], ((1,), (0,)))
        picked = picked.reshape(rows // piece, piece, feats).astype(bf16)
        if by_quarter:
            out_ref[q] = picked
        else:
            out_ref[:, q] = picked


def pick_rows(index, column, near, part, by_quarter, name):
    quarters, rows, _ = index.shape
    feats = column.shape[2] // 2
    piece = rows // near
    if by_quarter:
        block, place = (2, near, piece, feats), (lambda q: (q, 0, 0, 0))
        shape = (quarters, near, piece, feats)
    else:
        block, place = (near, 2, piece, feats), (lambda q: (0, q, 0, 0))
        shape = (near, quarters, piece, feats)
    return pl.pallas_call(
        functools.partial(pick_kernel, by_quarter),
        grid=(quarters // 2,),
        in_specs=[
            pl.BlockSpec((2, rows, 1), lambda q: (q, 0, 0)),
            pl.BlockSpec((2, column.shape[1], feats), lambda q: (q, 0, part)),
        ],
        out_specs=pl.BlockSpec(block, place),
        out_shape=jax.ShapeDtypeStruct(shape, bf16),
        compiler_params=pltpu.CompilerParams(vmem_limit_bytes=48 * MIB),
        name=name,
    )(index, column)


TRIANGLE = ((0, 3, 4), (1, 2, 5))


def triangle(which):
    first, places = 0, []
    for i in TRIANGLE[which]:
        places.append((i, first))
        first += 6 - i
    return places, first


def inner_kernel(recv_ref, west_ref, east_ref, rows_t_ref, low_ref, high_ref, rows_ref):
    near, quarters, piece, feats = recv_ref.shape
    own, hidden = west_ref.shape
    for q in range(quarters):
        rows_ref[q * own : (q + 1) * own] = (
            recv_ref[:, q].astype(f32).reshape(own, feats).astype(bf16)
        )
    side = quarters * own // 6
    lanes = hidden // 2
    for which, out, riding in ((0, low_ref, west_ref), (1, high_ref, east_ref)):
        places, blocks = triangle(which)
        for i, first in places:
            part = dot(rows_ref[i * side : (i + 1) * side], rows_ref[i * side :], ((1,), (1,)))
            out[:, first * side : (first + 6 - i) * side] = part.astype(bf16)
        end, base = blocks * side, which * lanes
        out[:, end : end + lanes] = riding[:side, base : base + lanes]
        end += lanes
        for j in range(2):
            spread = riding[side:, base + j * lanes // 2 : base + (j + 1) * lanes // 2]
            out[j * side // 2 : (j + 1) * side // 2, end : end + lanes // 2] = spread
    rows_t_ref[...] = rows_ref[...].T


def inner_products(recv, west, east):
    near, quarters, piece, feats = recv.shape
    own, hidden = west.shape
    side = quarters * own // 6
    packs = [
        jax.ShapeDtypeStruct((side, triangle(i)[1] * side + 3 * hidden // 4), bf16)
        for i in range(2)
    ]
    return pl.pallas_call(
        inner_kernel,
        out_shape=[pltpu.HBM((feats, quarters * own), bf16), *packs],
        scratch_shapes=[pltpu.VMEM((quarters * own, feats), bf16)],
        compiler_params=pltpu.CompilerParams(vmem_limit_bytes=20 * MIB),
        name="inner_products",
    )(recv, west, east)


def hidden_kernel(grads_ref, matrix_ref, out_act_ref, dw_act_ref, up_ref, dw_ref, hidden_ref):
    blocks, depth, width = matrix_ref.shape
    grads = jnp.concatenate([grads_ref[i] for i in range(grads_ref.shape[0])], axis=1)
    matrix = jnp.concatenate([matrix_ref[j] for j in range(blocks)], axis=1)
    share = dot(grads, matrix, ((1,), (0,)))

    @pl.when(pl.program_id(0) == 0)
    def _():
        hidden_ref[...] = share

    @pl.when(pl.program_id(0) == pl.num_programs(0) - 1)
    def _():
        dw = jnp.zeros((grads.shape[0], 1), f32)
        for j in range(blocks):
            lanes = slice(j * width, (j + 1) * width)
            hidden = hidden_ref[:, lanes] + share[:, lanes]
            up_ref[:, lanes] = (hidden * out_act_ref[j]).astype(bf16)
            dw = dw + jnp.sum(hidden * dw_act_ref[j], axis=1, keepdims=True)
        dw_ref[...] = dw


def hidden_step(grads, matrix, out_act, dw_act):
    parts, rows, feats = grads.shape
    blocks, depth, width = matrix.shape
    outs = [
        pltpu.HBM((rows, blocks * width), bf16),
        pltpu.HBM((rows, 1), f32),
    ]
    return pl.pallas_call(
        hidden_kernel,
        grid=(2,),
        in_specs=[
            pl.BlockSpec((parts // 2, rows, feats), lambda k: (k, 0, 0)),
            pl.BlockSpec((blocks, depth // 2, width), lambda k: (0, k, 0)),
            pl.BlockSpec(out_act.shape, lambda k: (0, 0, 0)),
            pl.BlockSpec(dw_act.shape, lambda k: (0, 0, 0)),
        ],
        out_specs=[pl.BlockSpec(out.shape, lambda k: (0, 0)) for out in outs],
        out_shape=outs,
        scratch_shapes=[pltpu.VMEM((rows, blocks * width), f32)],
        compiler_params=pltpu.CompilerParams(vmem_limit_bytes=53 * MIB),
        name="hidden_step",
    )(grads, matrix, out_act, dw_act)


def last_kernel(
    rank_ref, rows_t_hbm, own_hbm, low_a, low_b, high_a, high_b, west_hbm, east_hbm,
    far_low, far_high, out_ref,
    up_ref, inner_ref, carried_ref, gram_ref, square_ref, poly_ref, start_ref, rows_t_ref,
    low_ref, high_ref, sems, up_t_ref,
):
    rank = rank_ref[0]
    own = west_hbm.shape[0]
    slots, hidden = up_ref.shape
    feats = rows_t_ref.shape[0]
    side, lanes = slots // 6, hidden // 2
    near = rank + 1 - 2 * lax.rem(rank, 2)

    def owned(owner, first=0, rows=own):
        return pl.ds(pl.multiple_of(owner * own + first, 16), rows)

    moves = [
        (low_a, low_ref.at[0]),
        (low_b, low_ref.at[1]),
        (high_a, high_ref.at[0]),
        (high_b, high_ref.at[1]),
        (own_hbm, up_ref.at[owned(rank)]),
        (west_hbm, up_ref.at[owned(3 - rank)]),
        (east_hbm, up_ref.at[owned(near)]),
    ]
    for which, source in ((0, far_low), (1, far_high)):
        end, base = triangle(which)[1] * side, which * lanes
        place = up_ref.at[owned(3 - near, 0, side), pl.ds(base, lanes)]
        moves.append((source.at[:, pl.ds(end, lanes)], place))
        end += lanes
        for j in range(2):
            rows = pl.ds(j * side // 2, side // 2)
            place = pl.ds(base + j * lanes // 2, lanes // 2)
            place = up_ref.at[owned(3 - near, side, side // 2), place]
            moves.append((source.at[rows, pl.ds(end, lanes // 2)], place))
    moves.append((rows_t_hbm, rows_t_ref))
    copies = [
        pltpu.make_async_copy(source, place, sems.at[i])
        for i, (source, place) in enumerate(moves)
    ]
    for copy in copies:
        copy.start()
    for copy in copies[:4]:
        copy.wait()
    for which, packs in ((0, low_ref), (1, high_ref)):
        for i, first in triangle(which)[0]:
            at = slice(first * side, (first + 6 - i) * side)
            part = (packs[0, :, at].astype(f32) + packs[1, :, at].astype(f32)).astype(bf16)
            inner_ref[i * side : (i + 1) * side, i * side :] = part
            for j in range(i + 1, 6):
                block = part[:, (j - i) * side : (j - i + 1) * side].T
                inner_ref[j * side : (j + 1) * side, i * side : (i + 1) * side] = block
    for copy in copies[4:13]:
        copy.wait()
    up_t_ref[...] = up_ref[...].T
    norm = jnp.zeros((1, 1), f32)
    step = slots // 2
    for i in range(0, slots, step):
        carried = dot(inner_ref[i : i + step], up_ref[...], ((1,), (0,)))
        norm = norm + total(carried * up_ref[i : i + step].astype(f32))
        carried_ref[i : i + step] = carried.astype(bf16)
    scale = 1.0 / (1.01 * jnp.sqrt(jnp.maximum(norm, 0.0)) + 1e-07)
    step = hidden // 4
    for i in range(0, hidden, step):
        gram = dot(up_t_ref[i : i + step], carried_ref[:, i:], ((1,), (0,)))
        gram = (gram * scale * scale).astype(bf16)
        gram_ref[i : i + step, i:] = gram
        for j in range(i + step, hidden, step):
            gram_ref[j : j + step, i : i + step] = gram[:, j - i : j - i + step].T
    quartic = jnp.zeros((1, 1), f32)
    for i in range(0, hidden, step):
        square = dot(gram_ref[i : i + step], gram_ref[:, i:], ((1,), (0,)))
        quartic = quartic + 2.0 * total(square * square) - total(square[:, :step] * square[:, :step])
        square_ref[i : i + step, i:] = square
    rows = feats // 2
    copies[13].wait()
    for i in range(0, feats, rows):
        gradient = dot(rows_t_ref[i : i + rows], up_ref[...], ((1,), (0,)))
        start_ref[i : i + rows] = (gradient * scale).astype(bf16)
    bound = jnp.sqrt(jnp.sqrt(quartic)) + 1e-06
    first_scale = poly_third / bound
    second_scale = poly_fifth / (bound * bound)
    for i in range(0, hidden, step):
        poly = (
            first_scale * gram_ref[i : i + step, i:].astype(f32)
            + second_scale * square_ref[i : i + step, i:]
        ).astype(bf16)
        poly_ref[i : i + step, i:] = poly
        for j in range(i + step, hidden, step):
            poly_ref[j : j + step, i : i + step] = poly[:, j - i : j - i + step].T
    for i in range(0, feats, rows):
        start = start_ref[i : i + rows]
        mixed = dot(start, poly_ref[...], ((1,), (0,)))
        out_ref[0, i : i + rows] = (
            math.sqrt(D) * (poly_first * start.astype(f32) + mixed)
        ).astype(bf16)


def last_step(rank, rows_t, own, packs, ups):
    feats, slots = rows_t.shape
    hidden = own.shape[1]
    return pl.pallas_call(
        last_kernel,
        in_specs=[pl.BlockSpec(memory_space=pltpu.SMEM)]
        + [pl.BlockSpec(memory_space=pltpu.HBM)] * 10,
        out_shape=jax.ShapeDtypeStruct((1, feats, hidden), bf16),
        scratch_shapes=[
            pltpu.VMEM((slots, hidden), bf16),
            pltpu.VMEM((slots, slots), bf16),
            pltpu.VMEM((slots, hidden), bf16),
            pltpu.VMEM((hidden, hidden), bf16),
            pltpu.VMEM((hidden, hidden), f32),
            pltpu.VMEM((hidden, hidden), bf16),
            pltpu.VMEM((feats, hidden), bf16),
            pltpu.VMEM((feats, slots), bf16),
            pltpu.VMEM((2,) + packs[0].shape, bf16),
            pltpu.VMEM((2,) + packs[2].shape, bf16),
            pltpu.SemaphoreType.DMA((14,)),
            pltpu.VMEM((hidden, slots), bf16),
        ],
        compiler_params=pltpu.CompilerParams(vmem_limit_bytes=46 * MIB),
        name="last_step",
    )(rank, rows_t, own, *packs, *ups)


def on_device(tokens_in, out_grad, expert_ids, combine, down_weight, gate_saved, up_saved):
    nx, nz, nc = (lax.axis_size(name) for name in ("x", "z", "c"))
    ny = lax.axis_size("y")
    experts = nx * nz * nc
    near = nx * nc
    zl = nz // ny
    slots = experts * CAP
    own_slots = slots // ny
    tok_rows, top_count = expert_ids.shape
    feats = tokens_in.shape[1]
    hidden_part = gate_saved.shape[2]

    column = lax.all_gather(
        jnp.concatenate([tokens_in, out_grad], axis=1), "z", axis=0, tiled=True
    )

    flat_ids = expert_ids.reshape(-1)
    position = block_positions(flat_ids)
    is_live = flat_ids < experts
    ez = (flat_ids // nc) % nz
    exc = (flat_ids // (nc * nz)) * nc + flat_ids % nc
    target = jnp.where(is_live, (ez * near + exc) * CAP + position, -1)
    matches = target[None, :] == jnp.arange(slots, dtype=jnp.int32)[:, None]
    token_of = (jnp.arange(tok_rows * top_count, dtype=jnp.int32) // top_count).astype(f32) + 1.0
    index_send = jnp.sum(jnp.where(matches, token_of[None, :], 0.0), axis=1)
    weight_send = jnp.sum(
        jnp.where(matches, combine.astype(f32).reshape(1, -1), 0.0), axis=1
    )
    routes = lax.all_to_all(
        jnp.stack([index_send.reshape(nz, near * CAP), weight_send.reshape(nz, near * CAP)], 1),
        "z", 0, 0, tiled=True,
    )
    routes = routes.reshape(nz, 2, near, CAP)
    start = (jnp.arange(nz, dtype=jnp.int32) % zl * tok_rows).astype(f32)[:, None, None]
    index = jnp.where(routes[:, 0] > 0.0, routes[:, 0] + start, 0.0)
    index = index.reshape(ny, zl, near, CAP).transpose(0, 2, 1, 3).reshape(ny, own_slots, 1)
    weight = routes[:, 1].reshape(ny, zl, near, CAP).transpose(0, 2, 1, 3)
    weight = lax.dynamic_index_in_dim(weight, lax.axis_index("y"), 0, keepdims=False)
    weight = lax.all_to_all(weight.reshape(near, zl * CAP), ("x", "c"), 0, 0, tiled=True)
    weight = weight.reshape(own_slots)[:, None]

    row = jnp.arange(slots, dtype=jnp.int32)
    rest = row // CAP
    block = rest % zl
    rest = rest // zl
    row_c = rest % nc
    rest = rest // nc
    row_x = rest % nx
    row_q = rest // nx
    source = ((row_x * nz + row_q * zl + block) * nc + row_c) * CAP + row % CAP
    order = (source[:, None] == row[None, :]).astype(bf16)
    saved = jnp.concatenate([gate_saved[0], up_saved[0]], axis=1)
    saved = dot(order, saved, ((1,), (0,))).astype(bf16)
    matrix, saved = gather_weights(down_weight[0], saved)
    saved = lax.all_to_all(
        saved.reshape(ny, own_slots, 2 * hidden_part), "y", 0, 0, tiled=True
    )

    gate, up = saved[:, :, :hidden_part].astype(f32), saved[:, :, hidden_part:].astype(f32)
    act = jax.nn.silu(gate)
    out_act, dw_act = act * weight[None], act * up
    column, matrix, out_act, dw_act = lax.optimization_barrier((column, matrix, out_act, dw_act))
    column = column.reshape(ny, zl * tok_rows, 2 * feats)
    grad_send = pick_rows(index, column, near, 1, True, "pick_grads")
    token_send = pick_rows(index, column, near, 0, False, "pick_tokens")
    beside, across = (lambda i: i ^ 1), (lambda i: ny - 1 - i)

    grads = lax.all_to_all(
        grad_send.reshape(ny * near, zl * CAP, feats), ("y", "x", "c"), 0, 0, tiled=True
    ).reshape(ny, own_slots, feats)
    token_send, grads = lax.optimization_barrier((token_send, grads))
    up_own, slot_dw = hidden_step(grads, matrix, out_act, dw_act)
    west, east = swap(up_own, across), swap(up_own, beside)
    back = slot_dw.reshape(near, zl, CAP).transpose(1, 0, 2)
    back = jnp.pad(back, ((0, 0), (0, 0), (0, 128 - CAP)))
    back = lax.dynamic_update_slice(
        jnp.zeros((nz, near, 128), f32), back, (lax.axis_index("y") * zl, 0, 0)
    )

    rows = lax.all_to_all(
        token_send.reshape(near, nz * CAP, feats), ("x", "c"), 0, 0, tiled=True
    ).reshape(near, ny, zl * CAP, feats)
    west, east, back = lax.optimization_barrier((west, east, back))
    rows_t, low, high = inner_products(rows, west, east)
    low_near, high_near = swap(low, beside), swap(high, across)
    low_size, high_size = (triangle(i)[1] * (slots // 6) for i in range(2))
    low = low[:, :low_size] + low_near[:, :low_size]
    high = high[:, :high_size] + high_near[:, :high_size]
    packs = (low, swap(low, across), high, swap(high, beside))
    ups = (west, east, low_near, high_near)

    back, rows_t = lax.optimization_barrier((back, rows_t))
    back = lax.all_to_all(back, "z", 0, 0, tiled=True)[:, :, :CAP]
    back = back.transpose(1, 0, 2).reshape(1, near, nz * CAP)
    back = jnp.broadcast_to(back, (ny, near, nz * CAP)).reshape(ny * near, nz * CAP)
    back = lax.all_to_all(back, ("y", "x", "c"), 0, 0, tiled=True)

    rank = lax.axis_index("y").reshape(1)
    update = last_step(rank, rows_t, up_own, packs, ups)
    back, update = lax.optimization_barrier((back, update))
    back = jnp.sum(back.reshape(ny, near, nz, CAP), axis=0).transpose(1, 0, 2).reshape(-1)
    dcombine = jnp.sum(jnp.where(matches, back[:, None], 0.0), axis=0)
    dcombine = dcombine.reshape(tok_rows, top_count)
    return (update, dcombine)


def build(mesh, plane):
    split_mesh = Mesh(
        mesh.devices.reshape(plane + (mesh.devices.shape[1],)), ("x", "z", "c", "y")
    )
    expert = ("x", "z", "c")
    in_specs = (
        P(expert, "y"),
        P(expert, "y"),
        P(expert, None),
        P(expert, None),
        P(expert, "y", None),
        P(expert, None, "y"),
        P(expert, None, "y"),
    )
    out_specs = (P(expert, "y", None), P(expert, None))
    return jax.shard_map(
        on_device, mesh=split_mesh, in_specs=in_specs, out_specs=out_specs, check_vma=False
    )


def solution(mesh):
    return build(mesh, PLANE)
```
